32 devices in a mesh: seq: 4 (over z), fsdp: 8 (over y, x, core).
Axes of the slice: x: 2, y: 2, z: 4, core: 2. Of those that a mesh axis runs over, the one named last changes fastest.
Arguments:
- tokens: bfloat16 [8, 1024, 768], P('fsdp', 'seq'), may hold values from -6 to 6
- routes: int32 [8, 1024, 1], P('fsdp', 'seq'), may hold values from 0 to 1; in each aligned block of 256 rows (0 to 255, 256 to 511, ..., all dimensions but the last counted through in order) at most 144 rows name the same one
- buckets: int32 [2047], replicated, may hold values from 0 to 31
- gain_attn: float32 [768], replicated, may hold values from 0.1 to 1.9
- w_query: bfloat16 [768, 768], P('fsdp'), may hold values from -0.21875 to 0.21875
- w_key: bfloat16 [768, 768], P('fsdp'), may hold values from -0.21875 to 0.21875
- w_value: bfloat16 [768, 768], P('fsdp'), may hold values from -0.21875 to 0.21875
- w_out: bfloat16 [768, 768], P('fsdp'), may hold values from -3.5 to 3.5
- bias_table: float32 [32, 12], replicated, may hold values from -6 to 6
- gain_ff: float32 [768], replicated, may hold values from 0.1 to 1.9
- router: float32 [768, 2], replicated, may hold values from -0.15625 to 0.15625
- expert_up: bfloat16 [2, 3072, 768], P(None, ('seq', 'fsdp')), may hold values from -0.21875 to 0.21875
- expert_down: bfloat16 [2, 3072, 768], P(None, ('seq', 'fsdp')), may hold values from -0.3125 to 0.3125
- out_grad: bfloat16 [8, 1024, 768], P('fsdp', 'seq'), may hold values from -6 to 6
Outputs:
- output: bfloat16 [8, 1024, 768], P('fsdp', 'seq')
- tokens_grad: float32 [8, 1024, 768], P('fsdp', 'seq')
- gain_attn_grad: float32 [768], replicated
- w_query_grad: float32 [768, 768], P('fsdp')
- w_key_grad: float32 [768, 768], P('fsdp')
- w_value_grad: float32 [768, 768], P('fsdp')
- w_out_grad: float32 [768, 768], P('fsdp')
- bias_table_grad: float32 [32, 12], replicated
- gain_ff_grad: float32 [768], replicated
- router_grad: float32 [768, 2], replicated
- expert_up_grad: float32 [2, 3072, 768], P(None, ('seq', 'fsdp'))
- expert_down_grad: float32 [2, 3072, 768], P(None, ('seq', 'fsdp'))
The draws below stay inside these ranges and needn't reach their ends.
Inputs may be any that keep to these rules, and one draw needn't show every extreme that they name: `routes`: in each aligned block of 256 positions of a sequence, at most 144 tokens name one expert.
All inputs are finite; a program needn't handle non-finite values.
Results may differ from the reference program's by a relative error of at most 0.017.
Values may be sent and summed in bfloat16 or wider, within the bound.
No kernel may reach another device: no remote copies, remote signals or barrier semaphores. Data moves between devices by JAX's collectives and lax.ppermute only.
A program may use at most 192 MiB of HBM per device.

```python
import math
import jax
import jax.numpy as jnp
import numpy as np
from jax import lax

D = 768
FF = 3072
BUCKETS = 32
HEAD = 64
EXP = 2
LEN = 1024
HEADS = 12
BLOCK = 256
CAP = 144
SEQS = 8
N_SEQ = 4


def place_ends(drawn, own_key, low, largest):
    extent = drawn.shape
    place = [jax.random.randint(jax.random.fold_in(own_key, axis), (), 0, extent[axis]) for axis in range(len(extent))]
    drawn = drawn.at[tuple(place)].set(low)
    longest = extent.index(max(extent))
    place[longest] = (place[longest] + 1) % extent[longest]
    return drawn.at[tuple(place)].set(largest)


def block_scale(rng, extent, shards, low, high):
    level, own = 1.0, jax.random.fold_in(rng, 6)
    for axis_at, parts in shards:
        draws = jnp.exp(jax.random.uniform(jax.random.fold_in(own, axis_at), (parts,), jnp.float32, low / len(shards), high / len(shards)))
        level = level * jnp.repeat(draws, extent[axis_at] // parts).reshape([-1 if axis == axis_at else 1 for axis in range(len(extent))])
    return level


def routed_block(stream_key, own, number, rows, number_of, top, bound, skew):
    ranking = jax.random.permutation(stream_key, number_of)
    packed, common = shares(number_of, rows * top, bound, skew, True), shares(number_of, rows * top, bound, skew, False)
    places = jnp.arange(number_of)

    def named(sizes, turn):
        used = int((sizes > 0).sum())
        fixed = max(1, used // 4)
        passed = fixed + (places - fixed + turn * (used - fixed)) % max(1, number_of - fixed)
        return jnp.zeros((number_of,), jnp.int32).at[ranking[jnp.where(places < fixed, places, passed)]].set(jnp.asarray(sizes, jnp.int32))

    sizes = jnp.where(number % 4 == 0, named(packed, number // 4), named(common, number - number // 4 - 1))
    mixed = jax.random.permutation(jax.random.fold_in(own, 3), number_of)
    donor, taker = mixed[0:number_of // 2 * 2:2], mixed[1:number_of // 2 * 2:2]
    margin = jnp.minimum(sizes[donor] - 1, bound - sizes[taker]) // 2
    margin = jnp.where((donor == ranking[0]) | (taker == ranking[0]) | (sizes[taker] == 0), 0, jnp.maximum(margin, 0))
    passed = jax.random.randint(jax.random.fold_in(own, 4), (number_of // 2,), 0, 1 << 20) % (margin + 1)
    sizes = sizes.at[donor].add(-passed).at[taker].add(passed)
    items = jnp.searchsorted(jnp.cumsum(sizes), jnp.arange(rows * top), side="right").astype(jnp.int32)
    grid = items.reshape(top, rows).T
    grid = grid[jax.random.permutation(jax.random.fold_in(own, 1), rows)]
    turn = jax.random.randint(jax.random.fold_in(own, 2), (rows, 1), 0, top)
    return jnp.take_along_axis(grid, (jnp.arange(top)[None, :] + turn) % top, axis=1)


def shares(amount, total, limit, lean, full):
    loads = [(1 << 20) // math.isqrt(rank ** lean) + 1 for rank in range(1, amount + 1)]
    largest = limit if full else min(limit, max(-(-total // amount), total * loads[0] // sum(loads)))
    least = 1 if total - largest >= amount - 1 else 0
    holding, spare = [largest] + [least] * (amount - 1), total - largest - least * (amount - 1)
    while spare > 0:
        movable = [i for i in range(1, amount) if holding[i] < largest] or [i for i in range(1, amount) if holding[i] < limit]
        whole, left = sum([loads[i] for i in movable]), spare
        for i in movable:
            more = min(limit - holding[i], max(1, left * loads[i] // whole), spare)
            holding[i] = holding[i] + more
            spare = spare - more
    return np.array(holding)


def centred(key, dims, spread, limit, cuts=(), kind=jnp.bfloat16):
    drawn = jax.random.normal(key, dims, jnp.float32) * spread
    if len(cuts) > 0:
        drawn = block_scale(key, dims, cuts, -0.22, 0.18) * drawn
    return jnp.clip(drawn, min=-limit, max=limit).astype(kind)


def setup_inputs(seed: int = 0) -> dict:
    seeds = jax.random.split(jax.random.key(seed), 15)
    tokens = centred(seeds[0], (SEQS, LEN, D), 1.0, 6.0, ((0, 8), (1, 4)))
    routes_keys = jax.random.split(jax.random.fold_in(seeds[1], 1), SEQS * LEN // BLOCK)
    routes_turns = jax.random.permutation(jax.random.fold_in(seeds[1], 3), SEQS * LEN // BLOCK)
    routes = jax.vmap(lambda own, number: routed_block(jax.random.fold_in(seeds[1], 2), own, number, BLOCK, EXP, 1, CAP, 0))(routes_keys, routes_turns).reshape((SEQS, LEN, 1))
    buckets = place_ends(jax.random.randint(seeds[2], (2 * LEN - 1,), 0, BUCKETS), jax.random.fold_in(seeds[2], 1), 0, BUCKETS - 1).astype(jnp.int32)
    gain_attn = jnp.clip(1.0 + 0.18 * jax.random.normal(seeds[3], (D,), jnp.float32), 0.1, 1.9)
    w_query = centred(seeds[4], (D, D), D ** -0.5, 0.21875, ((0, 8),))
    w_key = centred(seeds[5], (D, D), D ** -0.5, 0.21875, ((0, 8),))
    w_value = centred(seeds[6], (D, D), D ** -0.5, 0.21875, ((0, 8),))
    w_out = centred(seeds[7], (D, D), (max(D // 256, 1)) ** -0.5, 3.5, ((0, 8),))
    bias_table = centred(seeds[8], (BUCKETS, HEADS), 1.0, 6.0, (), jnp.float32)
    gain_ff = jnp.clip(1.0 + 0.18 * jax.random.normal(seeds[9], (D,), jnp.float32), 0.1, 1.9)
    router = centred(seeds[10], (D, EXP), (2 * D) ** -0.5, 0.15625, (), jnp.float32)
    expert_up = centred(seeds[11], (EXP, FF, D), D ** -0.5, 0.21875, ((1, 32),))
    expert_down = centred(seeds[12], (EXP, FF, D), (FF // 8) ** -0.5, 0.3125, ((1, 32),))
    out_grad = centred(seeds[13], (SEQS, LEN, D), 1.0, 6.0, ((0, 8), (1, 4)))
    return dict(tokens=tokens, routes=routes, buckets=buckets, gain_attn=gain_attn, w_query=w_query, w_key=w_key, w_value=w_value, w_out=w_out, bias_table=bias_table, gain_ff=gain_ff, router=router, expert_up=expert_up, expert_down=expert_down, out_grad=out_grad)


PRECISE = lax.Precision.HIGHEST
EPSILON = 1e-06

@jax.custom_vjp
def low(v):
    return lax.optimization_barrier(v.astype(jnp.bfloat16)).astype(jnp.float32)

@jax.custom_vjp
def low_back(v):
    return v

def low_keep(v):
    return (low(v), None)

def low_pass(kept, grad):
    return (grad,)

def back_keep(v):
    return (v, None)

def back_low(kept, grad):
    return (low(grad),)
low.defvjp(low_keep, low_pass)
low_back.defvjp(back_keep, back_low)

def norm_scale(values):
    return lax.rsqrt(lax.optimization_barrier(jnp.mean(values * values, axis=-1, keepdims=True)) + EPSILON)

def block_layer(tokens, routes, buckets, gain_attn, w_query, w_key, w_value, w_out, bias_table, gain_ff, router, expert_up, expert_down):
    positions = jnp.arange(LEN).astype(jnp.int32)
    offsets = (positions[None, :] - positions[:, None] + (LEN - 1)).astype(jnp.int32)
    position_bias = jnp.transpose(bias_table[buckets[offsets]], (2, 0, 1))
    head_count = D // HEAD

    def one_sequence(seq_pair):
        values, chosen = seq_pair
        normed = low(values * norm_scale(values) * gain_attn)

        def project(weight):
            return low_back(low(jnp.dot(normed, weight, precision=PRECISE))).reshape(LEN, head_count, HEAD)
        query = project(w_query)
        keys_all = project(w_key)
        values_all = project(w_value)
        raw_scores = jnp.einsum('ihd,jhd->hij', query, keys_all, precision=PRECISE)
        scores = low_back(raw_scores * HEAD ** (-0.5) + position_bias)
        weights = low(jax.nn.softmax(scores, axis=-1))
        context = jnp.einsum('hij,jhd->ihd', weights, values_all, precision=PRECISE).reshape(LEN, D)
        context = low_back(low(context))
        hidden = values + low_back(jnp.dot(context, w_out, precision=PRECISE))
        ffnorm = hidden * norm_scale(hidden) * gain_ff
        route_probs = jax.nn.softmax(jnp.dot(ffnorm, router, precision=PRECISE), axis=-1)
        picked = (chosen[:, None] == jnp.arange(EXP).astype(jnp.int32)[None, :]).astype(jnp.float32)
        gate_value = lax.optimization_barrier(jnp.sum(route_probs * picked, axis=-1))
        blocked = picked.reshape(N_SEQ, BLOCK, EXP)
        slot_number = lax.optimization_barrier(jnp.sum((jnp.cumsum(blocked, axis=1) - blocked) * blocked, axis=-1)).astype(jnp.int32)
        slot_index = chosen.reshape(N_SEQ, BLOCK) * CAP + slot_number
        dispatch = (slot_index[:, None, :] == jnp.arange(EXP * CAP).astype(jnp.int32)[None, :, None]).astype(jnp.float32)
        dispatched = jnp.einsum('bct,btd->bcd', dispatch, low(ffnorm).reshape(N_SEQ, BLOCK, D), precision=PRECISE)
        dispatched = dispatched.reshape(N_SEQ, EXP, CAP, D)
        pre_act = low_back(jnp.einsum('becd,efd->becf', dispatched, expert_up, precision=PRECISE))
        activated = low(jax.nn.gelu(pre_act, approximate=False))
        returned = low_back(jnp.einsum('becf,efd->becd', activated, expert_down, precision=PRECISE))
        returned = returned.reshape(N_SEQ, EXP * CAP, D)
        token_expert = jnp.einsum('bct,bcd->btd', dispatch, returned, precision=PRECISE).reshape(LEN, D)
        return hidden + gate_value[:, None] * token_expert
    return lax.map(jax.checkpoint(one_sequence), (tokens, routes[:, :, 0]))

def reference(tokens, routes, buckets, gain_attn, w_query, w_key, w_value, w_out, bias_table, gain_ff, router, expert_up, expert_down, out_grad):

    def forward(inputs, gain_one, query_weight, key_weight, value_weight, out_weight, table, gain_two, router_weight, up_weight, down_weight):
        return block_layer(inputs, routes, buckets, gain_one, query_weight, key_weight, value_weight, out_weight, table, gain_two, router_weight, up_weight, down_weight)
    result, pullback = jax.vjp(forward, tokens.astype(jnp.float32), gain_attn.astype(jnp.float32), w_query.astype(jnp.float32), w_key.astype(jnp.float32), w_value.astype(jnp.float32), w_out.astype(jnp.float32), bias_table.astype(jnp.float32), gain_ff.astype(jnp.float32), router.astype(jnp.float32), expert_up.astype(jnp.float32), expert_down.astype(jnp.float32))
    grads = pullback(out_grad.astype(jnp.float32))
    return (result.astype(jnp.bfloat16), grads[0], grads[1], grads[2], grads[3], grads[4], grads[5], grads[6], grads[7], grads[8], grads[9], grads[10])
```

```python
import jax
import jax.numpy as jnp
from jax import lax
from jax.experimental import pallas as pl
from jax.experimental.pallas import tpu as pltpu
from jax.sharding import PartitionSpec as P

HEAD = 64
EPSILON = 1e-06
PRECISE = lax.Precision.HIGHEST
ROOT_HALF = 0.7071067811865476
DENSITY = 0.3989422804014327
LOG2E = 1.4426950408889634
SCORE_SCALE = HEAD ** (-0.5)
VMEM_LIMIT = 56 * 1024 * 1024
BF16 = jnp.bfloat16
F32 = jnp.float32


def dot_of(left, right, left_dim, right_dim):
    return lax.dot_general(
        left, right, (((left_dim,), (right_dim,)), ((), ())), preferred_element_type=F32
    )


def norm_scale(values):
    return lax.rsqrt(jnp.mean(values * values, axis=-1, keepdims=True) + EPSILON)


def bias_tiles_kernel(reversed_ref, tiles_ref):
    rows = tiles_ref.shape[1]
    width = reversed_ref.shape[2]
    for head in range(tiles_ref.shape[0]):
        line = jnp.broadcast_to(reversed_ref[head], (rows, width))
        skewed = pltpu.roll(line, width - (rows - 1), 1, stride=1, stride_axis=0)
        tiles_ref[head] = skewed[:, : tiles_ref.shape[2]]


def bias_tiles(reversed_bias, rows, columns):
    heads = reversed_bias.shape[0]
    return pl.pallas_call(
        bias_tiles_kernel,
        out_shape=jax.ShapeDtypeStruct((heads, rows, columns), F32),
        in_specs=[pl.BlockSpec(memory_space=pltpu.VMEM)],
        out_specs=pl.BlockSpec(memory_space=pltpu.VMEM),
        compiler_params=pltpu.CompilerParams(vmem_limit_bytes=VMEM_LIMIT),
        name="bias_tiles",
    )(reversed_bias)


def tile_start(me, key_block, query_block, ways, rows):
    key_place = lax.rem(me + key_block, ways)
    query_place = lax.rem(me + query_block, ways)
    return pl.multiple_of((query_place - key_place + ways - 1) * rows, rows)


def attend_kernel(me_ref, qkv_ref, tiles_ref, context_ref, total_ref, context_t):
    heads, rows = tiles_ref.shape[0], tiles_ref.shape[1]
    length = qkv_ref.shape[1]
    ways = length // rows
    width = heads * HEAD
    me = me_ref[0]
    for head in range(heads):
        lanes = slice(head * HEAD, (head + 1) * HEAD)
        key_lanes = slice(width + head * HEAD, width + (head + 1) * HEAD)
        value_lanes = slice(2 * width + head * HEAD, 2 * width + (head + 1) * HEAD)

        def one_block(query_block, _):
            query_rows = pl.ds(pl.multiple_of(query_block * rows, rows), rows)
            query = qkv_ref[0, query_rows, lanes]
            scores = []
            for key_block in range(ways):
                key = qkv_ref[0, key_block * rows : (key_block + 1) * rows, key_lanes]
                start = tile_start(me, key_block, query_block, ways, rows)
                scores.append(
                    dot_of(key, query, 1, 1) * (SCORE_SCALE * LOG2E)
                    + tiles_ref[head, :, pl.ds(start, rows)]
                )
            top = scores[0]
            for tile in scores[1:]:
                top = jnp.maximum(top, tile)
            top = jnp.max(top, axis=0, keepdims=True)
            total = jnp.zeros((1, rows), F32)
            context = jnp.zeros((HEAD, rows), F32)
            for key_block in range(ways):
                value = qkv_ref[0, key_block * rows : (key_block + 1) * rows, value_lanes]
                shifted = jnp.exp2(scores[key_block] - top)
                total = total + jnp.sum(shifted, axis=0, keepdims=True)
                context = context + dot_of(value, shifted.astype(BF16), 0, 0)
            context_t[lanes, query_rows] = context / total
            total_ref[0, head, :, query_rows] = top + jnp.log2(total)
            return 0

        lax.fori_loop(0, ways, one_block, 0)
    context_ref[0] = context_t[...].T.astype(BF16)


def attend(me, qkv, tiles):
    seq_count, length, triple = qkv.shape
    heads, rows, columns = tiles.shape
    width = triple // 3
    return pl.pallas_call(
        attend_kernel,
        grid=(seq_count,),
        out_shape=(
            jax.ShapeDtypeStruct((seq_count, length, width), BF16),
            jax.ShapeDtypeStruct((seq_count, heads, 1, length), F32),
        ),
        in_specs=[
            pl.BlockSpec(memory_space=pltpu.SMEM),
            pl.BlockSpec((1, length, triple), lambda i: (i, 0, 0)),
            pl.BlockSpec((heads, rows, columns), lambda i: (0, 0, 0)),
        ],
        out_specs=(
            pl.BlockSpec((1, length, width), lambda i: (i, 0, 0)),
            pl.BlockSpec((1, heads, 1, length), lambda i: (i, 0, 0, 0)),
        ),
        scratch_shapes=[pltpu.VMEM((width, length), F32)],
        compiler_params=pltpu.CompilerParams(vmem_limit_bytes=VMEM_LIMIT),
        name="attend",
    )(me, qkv, tiles)


def attend_back_kernel(
    me_ref, qkv_ref, grad_ref, total_ref, tiles_ref, out_ref, offset_ref,
    query_t, key_sum, value_sum, tile_sum,
):
    heads, rows = tiles_ref.shape[0], tiles_ref.shape[1]
    length = qkv_ref.shape[1]
    ways = length // rows
    width = heads * HEAD
    me = me_ref[0]
    key_sum[...] = jnp.zeros(key_sum.shape, F32)
    value_sum[...] = jnp.zeros(value_sum.shape, F32)
    for head in range(heads):
        lanes = slice(head * HEAD, (head + 1) * HEAD)
        key_lanes = slice(width + head * HEAD, width + (head + 1) * HEAD)
        value_lanes = slice(2 * width + head * HEAD, 2 * width + (head + 1) * HEAD)
        tile_sum[...] = jnp.zeros(tile_sum.shape, F32)

        def one_block(query_block, _):
            query_rows = pl.ds(pl.multiple_of(query_block * rows, rows), rows)
            query = qkv_ref[0, query_rows, lanes]
            grad = grad_ref[0, query_rows, lanes]
            total = total_ref[0, head, :, query_rows]
            probs, weight_grads = [], []
            inner = jnp.zeros((1, rows), F32)
            for key_block in range(ways):
                key_rows = slice(key_block * rows, (key_block + 1) * rows)
                start = tile_start(me, key_block, query_block, ways, rows)
                scores = (
                    dot_of(qkv_ref[0, key_rows, key_lanes], query, 1, 1)
                    * (SCORE_SCALE * LOG2E)
                    + tiles_ref[head, :, pl.ds(start, rows)]
                )
                prob = jnp.exp2(scores - total)
                weight_grad = dot_of(qkv_ref[0, key_rows, value_lanes], grad, 1, 1)
                inner = inner + jnp.sum(prob * weight_grad, axis=0, keepdims=True)
                value_sum[key_rows, lanes] += dot_of(prob.astype(BF16), grad, 1, 0)
                probs.append(prob)
                weight_grads.append(weight_grad)
            query_grad = jnp.zeros((HEAD, rows), F32)
            for key_block in range(ways):
                key_rows = slice(key_block * rows, (key_block + 1) * rows)
                start = tile_start(me, key_block, query_block, ways, rows)
                score_grad = probs[key_block] * (weight_grads[key_block] - inner)
                tile_sum[:, pl.ds(start, rows)] += score_grad
                score_low = score_grad.astype(BF16)
                key_sum[key_rows, lanes] += dot_of(score_low, query, 1, 0)
                query_grad = query_grad + dot_of(
                    qkv_ref[0, key_rows, key_lanes], score_low, 0, 0
                )
            query_t[lanes, query_rows] = query_grad
            return 0

        lax.fori_loop(0, ways, one_block, 0)
        folded, half = tile_sum[...], rows // 2
        while half:
            folded = pltpu.roll(folded[:half], half, 1) + folded[half:]
            half //= 2
        offset_ref[0, head] = folded
    out_ref[0, :, :width] = (query_t[...].T * SCORE_SCALE).astype(BF16)
    out_ref[0, :, width : 2 * width] = (key_sum[...] * SCORE_SCALE).astype(BF16)
    out_ref[0, :, 2 * width :] = value_sum[...].astype(BF16)


def attend_back(me, qkv, grads, totals, tiles, span):
    seq_count, length, triple = qkv.shape
    heads, rows, columns = tiles.shape
    width = triple // 3
    return pl.pallas_call(
        attend_back_kernel,
        grid=(seq_count,),
        out_shape=(
            jax.ShapeDtypeStruct((seq_count, length, triple), BF16),
            jax.ShapeDtypeStruct((seq_count, heads, 1, span), F32),
        ),
        in_specs=[
            pl.BlockSpec(memory_space=pltpu.SMEM),
            pl.BlockSpec((1, length, triple), lambda i: (i, 0, 0)),
            pl.BlockSpec((1, length, width), lambda i: (i, 0, 0)),
            pl.BlockSpec((1, heads, 1, length), lambda i: (i, 0, 0, 0)),
            pl.BlockSpec((heads, rows, columns), lambda i: (0, 0, 0)),
        ],
        out_specs=(
            pl.BlockSpec((1, length, triple), lambda i: (i, 0, 0)),
            pl.BlockSpec((1, heads, 1, span), lambda i: (i, 0, 0, 0)),
        ),
        scratch_shapes=[
            pltpu.VMEM((width, length), F32),
            pltpu.VMEM((length, width), F32),
            pltpu.VMEM((length, width), F32),
            pltpu.VMEM((rows, span), F32),
        ],
        compiler_params=pltpu.CompilerParams(vmem_limit_bytes=VMEM_LIMIT),
        name="attend_back",
    )(me, qkv, grads, totals, tiles)


def experts_kernel(slots_ref, grads_ref, weights_ref, out_ref, slot_grad_ref, weight_grad_ref):
    units = weights_ref.shape[0] * weights_ref.shape[4]
    model_width = weights_ref.shape[5]
    up = weights_ref[:, 0, 0, 0].reshape(units, model_width)
    down = weights_ref[:, 0, 1, 0].reshape(units, model_width)
    slots = slots_ref[0]
    grads = grads_ref[0]
    pre = dot_of(slots, up, 1, 1)
    normal_cdf = 0.5 * (1.0 + lax.erf(pre * ROOT_HALF))
    act = (pre * normal_cdf).astype(BF16)
    slope = normal_cdf + pre * jnp.exp(-0.5 * pre * pre) * DENSITY
    act_grad = dot_of(grads, down, 1, 1)
    pre_grad = (act_grad * slope).astype(BF16)
    returned = dot_of(act, down, 1, 0)
    back = dot_of(pre_grad, up, 1, 0)
    first = pl.program_id(1) == 0

    @pl.when(first)
    def _():
        out_ref[0] = returned
        slot_grad_ref[0] = back

    @pl.when(jnp.logical_not(first))
    def _():
        out_ref[0] += returned
        slot_grad_ref[0] += back

    part_shape = weight_grad_ref.shape[0:1] + weight_grad_ref.shape[4:]
    weight_grad_ref[:, 0, 0, 0] = dot_of(pre_grad, slots, 0, 0).astype(BF16).reshape(part_shape)
    weight_grad_ref[:, 0, 1, 0] = dot_of(act, grads, 0, 0).astype(BF16).reshape(part_shape)


def experts(slots, grads, weights):
    expert_count, rows, model_width = slots.shape
    shards, groups, kinds, _, units, _ = weights.shape
    row_spec = pl.BlockSpec((1, rows, model_width), lambda e, j: (e, 0, 0))
    weight_spec = pl.BlockSpec(
        (shards, 1, kinds, 1, units, model_width), lambda e, j: (0, j, 0, e, 0, 0)
    )
    flops = 12 * expert_count * rows * model_width * shards * groups * units
    return pl.pallas_call(
        experts_kernel,
        grid=(expert_count, groups),
        out_shape=(
            jax.ShapeDtypeStruct(slots.shape, F32),
            jax.ShapeDtypeStruct(slots.shape, F32),
            jax.ShapeDtypeStruct(weights.shape, BF16),
        ),
        in_specs=[row_spec, row_spec, weight_spec],
        out_specs=(row_spec, row_spec, weight_spec),
        compiler_params=pltpu.CompilerParams(vmem_limit_bytes=VMEM_LIMIT),
        cost_estimate=pl.CostEstimate(
            flops=flops, bytes_accessed=4 * weights.size, transcendentals=0
        ),
        name="experts",
    )(slots, grads, weights)


def turned(values, axis_name, step):
    ways = lax.axis_size(axis_name)
    return lax.ppermute(values, axis_name, [((i + step) % ways, i) for i in range(ways)])


def flipped(values, axis_name, bit):
    ways = lax.axis_size(axis_name)
    return lax.ppermute(values, axis_name, [(i, i ^ (1 << bit)) for i in range(ways)])


def sum_everywhere(values, axis_names):
    for axis_name in axis_names:
        for bit in range(lax.axis_size(axis_name).bit_length() - 1):
            values = values + flipped(values, axis_name, bit)
    return values


def cyclic(values, me, ways, axis, direction):
    size = values.shape[axis] // ways
    return jnp.concatenate(
        [
            lax.dynamic_slice_in_dim(
                values, lax.rem(me + direction * r + ways, ways) * size, size, axis
            )
            for r in range(ways)
        ],
        axis=axis,
    )


def shards(
    tokens,
    routes,
    buckets,
    gain_attn,
    w_query,
    w_key,
    w_value,
    w_out,
    bias_table,
    gain_ff,
    router,
    expert_up,
    expert_down,
    out_grad,
):
    seq_count, block_rows, model_width = tokens.shape
    ways = lax.axis_size("seq")
    group = lax.axis_size("fsdp")
    me = lax.axis_index("seq")
    length = block_rows * ways
    capacity = block_rows * 9 // 16
    expert_count = router.shape[1]
    token_rows = seq_count * block_rows
    slot_rows = seq_count * capacity
    width = model_width // ways
    local_heads = width // HEAD
    places = jnp.full((1,), me, jnp.int32)

    inputs_all = jnp.concatenate([tokens] + [turned(tokens, "seq", r) for r in range(1, ways)], axis=1)

    def columns_of(place):
        return jnp.concatenate(
            [
                lax.dynamic_slice_in_dim(weight, place * width, width, 1)
                for weight in (w_query, w_key, w_value)
            ],
            axis=1,
        )

    own_columns = lax.all_gather(columns_of(me), "fsdp", axis=0, tiled=True)

    own_experts = jnp.stack([expert_up, expert_down])
    far_experts = flipped(own_experts, "seq", 1)
    expert_weights = lax.all_gather(jnp.stack([own_experts, far_experts]), "fsdp", axis=0)
    full_out = lax.all_gather(w_out, "fsdp", axis=0, tiled=True)
    out_cyclic = cyclic(full_out, me, ways, 0, -1)
    rest_columns = lax.all_gather(
        jnp.concatenate([columns_of(lax.rem(me - r + ways, ways)) for r in range(1, ways)], axis=1),
        "fsdp",
        axis=0,
        tiled=True,
    )

    chosen = routes[:, :, 0]
    picked = (chosen[:, :, None] == jnp.arange(expert_count)[None, None, :]).astype(F32)
    earlier = jnp.cumsum(picked, axis=1) - picked
    slot_number = jnp.sum(earlier * picked, axis=-1).astype(jnp.int32)
    slot_index = chosen * capacity + slot_number
    dispatch = (
        slot_index[:, None, :] == jnp.arange(expert_count * capacity)[None, :, None]
    ).reshape(seq_count, expert_count, capacity, block_rows)
    dispatch_low = dispatch.astype(BF16)

    def to_slots(values):
        placed = jnp.einsum("nect,ntd->encd", dispatch_low, values, preferred_element_type=F32)
        return placed.astype(BF16).reshape(expert_count, slot_rows, model_width)

    def from_slots(values):
        return jnp.einsum(
            "nect,encd->ntd",
            dispatch_low,
            values.astype(BF16).reshape(expert_count, seq_count, capacity, model_width),
            preferred_element_type=F32,
        )

    grad_slots = to_slots(out_grad)
    far_grad_slots = flipped(grad_slots, "seq", 0)

    table_here = lax.dynamic_slice_in_dim(bias_table, me * local_heads, local_heads, 1)
    bucket_table = (buckets[:, None] == jnp.arange(bias_table.shape[0])[None, :]).astype(F32)
    reversed_buckets = jnp.pad(bucket_table[::-1], ((0, 1), (0, 0)))
    reversed_bias = jnp.einsum(
        "uk,kh->hu", reversed_buckets, table_here * LOG2E, precision=PRECISE
    )
    tiles = bias_tiles(reversed_bias[:, None, :], block_rows, length * 2 - block_rows)

    wide_inputs = inputs_all.astype(F32)
    scale_all = norm_scale(wide_inputs)
    normed_all = (wide_inputs * scale_all * gain_attn).astype(BF16)
    qkv = jnp.einsum("ntd,de->nte", normed_all, own_columns, preferred_element_type=F32).astype(BF16)
    contexts, totals = attend(places, qkv, tiles)

    def block_of(values, r):
        return values[:, r * block_rows : (r + 1) * block_rows]

    context_tokens = jnp.concatenate(
        [block_of(contexts, 0)]
        + [turned(block_of(contexts, r), "seq", -r) for r in range(1, ways)],
        axis=2,
    )
    context_rows = context_tokens.reshape(token_rows, model_width)
    attn_branch = jnp.dot(context_rows, out_cyclic, preferred_element_type=F32)
    inputs = tokens.astype(F32)
    first_scale = norm_scale(inputs)
    hidden = inputs + attn_branch.reshape(seq_count, block_rows, model_width)
    second_scale = norm_scale(hidden)
    ffnorm = hidden * second_scale * gain_ff
    logits = jnp.einsum("std,de->ste", ffnorm, router, precision=PRECISE)
    route_probs = jax.nn.softmax(logits, axis=-1)
    gate_value = jnp.sum(route_probs * picked, axis=-1)

    slots = to_slots(ffnorm.astype(BF16))
    gate_slots = jnp.einsum(
        "nect->enc", jnp.where(dispatch, gate_value[:, None, None, :], 0.0)
    ).reshape(expert_count, slot_rows)
    far_slots = flipped(slots, "seq", 0)
    far_gate_slots = flipped(gate_slots, "seq", 0)
    all_slots = jnp.concatenate([slots, far_slots], axis=1)
    all_grad_slots = jnp.concatenate([grad_slots, far_grad_slots], axis=1).astype(F32)
    all_gates = jnp.concatenate([gate_slots, far_gate_slots], axis=1)
    gated_grads = (all_grad_slots * all_gates[:, :, None]).astype(BF16)
    returned, slot_back, weight_parts = experts(all_slots, gated_grads, expert_weights)
    gate_parts = jnp.sum(returned * all_grad_slots, axis=-1)
    gate_grad_slots = gate_parts[:, :slot_rows] + flipped(gate_parts[:, slot_rows:], "seq", 0)
    slot_sum = slot_back[:, :slot_rows] + flipped(
        slot_back[:, slot_rows:].astype(BF16), "seq", 0
    ).astype(F32)
    returned_sum = returned[:, :slot_rows] + flipped(
        returned[:, slot_rows:].astype(BF16), "seq", 0
    ).astype(F32)

    output = (hidden + gate_value[:, :, None] * from_slots(returned_sum)).astype(BF16)
    upstream = out_grad.astype(F32)
    gate_grad = jnp.sum(
        jnp.where(
            dispatch,
            gate_grad_slots.reshape(expert_count, seq_count, capacity).transpose(1, 0, 2)[..., None],
            0.0,
        ),
        axis=(1, 2),
    )
    logit_grad = gate_value[:, :, None] * (picked - route_probs) * gate_grad[:, :, None]
    ffnorm_grad = from_slots(slot_sum) + jnp.einsum(
        "ste,de->std", logit_grad, router, precision=PRECISE
    )
    router_grad = jnp.einsum("std,ste->de", ffnorm, logit_grad, precision=PRECISE)
    weighted = ffnorm_grad * gain_ff
    inner_sum = jnp.mean(weighted * hidden, axis=-1, keepdims=True)
    hidden_grad = (
        upstream + second_scale * weighted - hidden * (second_scale**3) * inner_sum
    )
    gain_ff_grad = jnp.sum(ffnorm_grad * hidden * second_scale, axis=(0, 1))
    branch_grad = hidden_grad.astype(BF16).reshape(token_rows, model_width)
    context_grad = dot_of(branch_grad, out_cyclic, 1, 1).astype(BF16)
    context_grad = context_grad.reshape(seq_count, block_rows, model_width)
    context_grads = jnp.concatenate(
        [context_grad[:, :, :width]]
        + [
            turned(context_grad[:, :, r * width : (r + 1) * width], "seq", r)
            for r in range(1, ways)
        ],
        axis=1,
    )
    out_weight_grad = cyclic(dot_of(context_rows, branch_grad, 0, 0).astype(BF16), me, ways, 0, -1)

    qkv_grads, offset_grads = attend_back(places, qkv, context_grads, totals, tiles, 2 * length)
    own_grads = [block_of(qkv_grads, 0)] + [
        turned(block_of(qkv_grads, r), "seq", -r) for r in range(1, ways)
    ]
    column_grad = jnp.einsum("ntd,nte->de", normed_all, qkv_grads, preferred_element_type=F32)
    gain_attn_part = jnp.sum(column_grad * own_columns.astype(F32), axis=1) / gain_attn
    column_share = lax.psum_scatter(
        column_grad.astype(BF16), "fsdp", scatter_dimension=0, tiled=True
    )
    own_grads = jnp.concatenate(own_grads, axis=2)
    all_columns = jnp.concatenate([own_columns, rest_columns], axis=1)
    normed_grad = jnp.einsum("nte,de->ntd", own_grads, all_columns, preferred_element_type=F32)
    weighted = normed_grad * gain_attn
    inner_sum = jnp.mean(weighted * inputs, axis=-1, keepdims=True)
    tokens_grad = (
        hidden_grad + first_scale * weighted - inputs * (first_scale**3) * inner_sum
    )

    table_part = jnp.einsum(
        "uk,hu->kh", reversed_buckets, jnp.sum(offset_grads, axis=(0, 2)), precision=PRECISE
    )
    table_full = lax.dynamic_update_slice_in_dim(
        jnp.zeros(bias_table.shape, F32), table_part, me * local_heads, 1
    )
    small = jnp.concatenate(
        [gain_attn_part, gain_ff_grad, router_grad.reshape(-1), table_full.reshape(-1)]
    )
    small = sum_everywhere(small, ("fsdp", "seq"))
    gain_attn_sum = small[:model_width]
    gain_ff_sum = small[model_width : 2 * model_width]
    router_sum = small[2 * model_width : 2 * model_width + router.size].reshape(router.shape)
    table_sum = small[2 * model_width + router.size :].reshape(bias_table.shape)

    units = expert_up.shape[1]
    expert_share = lax.psum_scatter(weight_parts, "fsdp", scatter_dimension=0, tiled=True)[0]
    expert_sum = expert_share[0].astype(F32) + flipped(expert_share[1], "seq", 1).astype(F32)
    out_share = lax.psum_scatter(out_weight_grad, "fsdp", scatter_dimension=0, tiled=True)
    out_shares = [out_share] + [turned(out_share, "seq", r) for r in range(1, ways)]
    out_sum = sum(share.astype(F32) for share in out_shares)
    column_shares = jnp.concatenate(
        [column_share] + [turned(column_share, "seq", r) for r in range(1, ways)], axis=1
    )
    column_shares = cyclic(column_shares, ways - me, ways, 1, 1).astype(F32)
    column_shares = column_shares.reshape(-1, ways, 3, width)
    attn_sums = [column_shares[:, :, kind].reshape(-1, model_width) for kind in range(3)]
    return (
        output,
        tokens_grad,
        gain_attn_sum,
        attn_sums[0],
        attn_sums[1],
        attn_sums[2],
        out_sum,
        table_sum,
        gain_ff_sum,
        router_sum,
        expert_sum[0],
        expert_sum[1],
    )


def solution(mesh):
    in_specs = (
        P("fsdp", "seq", None),
        P("fsdp", "seq", None),
        P(),
        P(),
        P("fsdp", None),
        P("fsdp", None),
        P("fsdp", None),
        P("fsdp", None),
        P(),
        P(),
        P(),
        P(None, ("seq", "fsdp"), None),
        P(None, ("seq", "fsdp"), None),
        P("fsdp", "seq", None),
    )
    out_specs = (
        P("fsdp", "seq", None),
        P("fsdp", "seq", None),
        P(),
        P("fsdp", None),
        P("fsdp", None),
        P("fsdp", None),
        P("fsdp", None),
        P(),
        P(),
        P(),
        P(None, ("seq", "fsdp"), None),
        P(None, ("seq", "fsdp"), None),
    )
    return jax.shard_map(shards, mesh=mesh, in_specs=in_specs, out_specs=out_specs, check_vma=False)
```

```python
import jax
import jax.numpy as jnp
from jax import lax
from jax.experimental import pallas as pl
from jax.experimental.pallas import tpu as pltpu
from jax.sharding import PartitionSpec as P

HEAD = 64
EPSILON = 1e-06
PRECISE = lax.Precision.HIGHEST
ROOT_HALF = 0.7071067811865476
DENSITY = 0.3989422804014327
LOG2E = 1.4426950408889634
SCORE_SCALE = HEAD ** (-0.5)
VMEM_LIMIT = 56 * 1024 * 1024
BF16 = jnp.bfloat16
F32 = jnp.float32


def dot_of(left, right, left_dim, right_dim):
    return lax.dot_general(
        left, right, (((left_dim,), (right_dim,)), ((), ())), preferred_element_type=F32
    )


def kernel_cost(microseconds):
    return pl.CostEstimate(
        flops=int(microseconds * 8e7), bytes_accessed=int(microseconds * 3e5), transcendentals=0
    )


def norm_scale(values):
    return lax.rsqrt(jnp.mean(values * values, axis=-1, keepdims=True) + EPSILON)


def bias_tiles_kernel(reversed_ref, tiles_ref):
    rows = tiles_ref.shape[1]
    width = reversed_ref.shape[2]
    for head in range(tiles_ref.shape[0]):
        line = jnp.broadcast_to(reversed_ref[head], (rows, width))
        skewed = pltpu.roll(line, width - (rows - 1), 1, stride=1, stride_axis=0)
        tiles_ref[head] = skewed[:, : tiles_ref.shape[2]]


def bias_tiles(reversed_bias, rows, columns):
    heads = reversed_bias.shape[0]
    return pl.pallas_call(
        bias_tiles_kernel,
        out_shape=jax.ShapeDtypeStruct((heads, rows, columns), F32),
        in_specs=[pl.BlockSpec(memory_space=pltpu.VMEM)],
        out_specs=pl.BlockSpec(memory_space=pltpu.VMEM),
        compiler_params=pltpu.CompilerParams(vmem_limit_bytes=VMEM_LIMIT),
        cost_estimate=kernel_cost(4),
        name="bias_tiles",
    )(reversed_bias)


def tile_start(me, key_block, query_block, ways, rows):
    key_place = lax.rem(me + key_block, ways)
    query_place = lax.rem(me + query_block, ways)
    return pl.multiple_of((query_place - key_place + ways - 1) * rows, rows)


def project_kernel(*refs):
    columns_ref, gain_ref, normed_ref, qkv_ref = refs[-4:]
    rows = refs[0].shape[1]
    columns = columns_ref[...].T
    for r, block_ref in enumerate(refs[:-4]):
        values = block_ref[0].astype(F32)
        normed = (values * norm_scale(values) * gain_ref[...]).astype(BF16)
        normed_ref[0, r * rows : (r + 1) * rows] = normed
        qkv_ref[0, :, r * rows : (r + 1) * rows] = dot_of(columns, normed, 1, 1).astype(BF16)


def project(blocks, columns, gain):
    seq_count, rows, model_width = blocks[0].shape
    length = rows * len(blocks)
    triple = columns.shape[1]
    return pl.pallas_call(
        project_kernel,
        grid=(seq_count,),
        out_shape=(
            jax.ShapeDtypeStruct((seq_count, length, model_width), BF16),
            jax.ShapeDtypeStruct((seq_count, triple, length), BF16),
        ),
        in_specs=[pl.BlockSpec((1, rows, model_width), lambda i: (i, 0, 0))] * len(blocks)
        + [
            pl.BlockSpec((model_width, triple), lambda i: (0, 0)),
            pl.BlockSpec((1, model_width), lambda i: (0, 0)),
        ],
        out_specs=(
            pl.BlockSpec((1, length, model_width), lambda i: (i, 0, 0)),
            pl.BlockSpec((1, triple, length), lambda i: (i, 0, 0)),
        ),
        compiler_params=pltpu.CompilerParams(vmem_limit_bytes=VMEM_LIMIT),
        cost_estimate=kernel_cost(5),
        name="project",
    )(*blocks, columns, gain)


def attend_kernel(me_ref, qkv_ref, tiles_ref, *refs):
    context_refs, total_ref, keys = refs[:-2], refs[-2], refs[-1]
    heads, rows = tiles_ref.shape[0], tiles_ref.shape[1]
    ways = len(context_refs)
    me = me_ref[0]
    for head in range(heads):
        first = 3 * head * HEAD
        keys[head] = qkv_ref[0, first + HEAD : first + 2 * HEAD].T
    for query_block in range(ways):
        query_rows = slice(query_block * rows, (query_block + 1) * rows)
        starts = [tile_start(me, place, query_block, ways, rows) for place in range(ways)]
        for head in range(heads):
            first = 3 * head * HEAD
            query = qkv_ref[0, first : first + HEAD, query_rows]
            scores = [
                dot_of(keys[head, place * rows : (place + 1) * rows], query, 1, 0)
                * (SCORE_SCALE * LOG2E)
                + tiles_ref[head, :, pl.ds(starts[place], rows)]
                for place in range(ways)
            ]
            top = scores[0]
            for tile in scores[1:]:
                top = jnp.maximum(top, tile)
            top = jnp.max(top, axis=0, keepdims=True)
            total = jnp.zeros((1, rows), F32)
            context = jnp.zeros((HEAD, rows), F32)
            for place in range(ways):
                value = qkv_ref[
                    0, first + 2 * HEAD : first + 3 * HEAD, place * rows : (place + 1) * rows
                ]
                shifted = jnp.exp2(scores[place] - top)
                total = total + jnp.sum(shifted, axis=0, keepdims=True)
                context = context + dot_of(value, shifted.astype(BF16), 1, 0)
            context_refs[query_block][0, head * HEAD : (head + 1) * HEAD] = (
                context / total
            ).astype(BF16)
            total_ref[0, head, :, query_rows] = top + jnp.log2(total)


def attend(me, qkv, tiles):
    seq_count, triple, length = qkv.shape
    heads, rows, columns = tiles.shape
    width, ways = triple // 3, length // rows
    results = pl.pallas_call(
        attend_kernel,
        grid=(seq_count,),
        out_shape=[jax.ShapeDtypeStruct((seq_count, width, rows), BF16)] * ways
        + [jax.ShapeDtypeStruct((seq_count, heads, 1, length), F32)],
        in_specs=[
            pl.BlockSpec(memory_space=pltpu.SMEM),
            pl.BlockSpec((1, triple, length), lambda i: (i, 0, 0)),
            pl.BlockSpec((heads, rows, columns), lambda i: (0, 0, 0)),
        ],
        out_specs=[pl.BlockSpec((1, width, rows), lambda i: (i, 0, 0))] * ways
        + [pl.BlockSpec((1, heads, 1, length), lambda i: (i, 0, 0, 0))],
        scratch_shapes=[pltpu.VMEM((heads, length, HEAD), BF16)],
        compiler_params=pltpu.CompilerParams(vmem_limit_bytes=VMEM_LIMIT),
        cost_estimate=kernel_cost(11),
        name="attend",
    )(me, qkv, tiles)
    return results[:ways], results[ways]


def attend_back_kernel(me_ref, qkv_ref, *refs):
    ways = qkv_ref.shape[2] // refs[0].shape[2]
    grad_refs = refs[:ways]
    total_ref, tiles_ref = refs[ways : ways + 2]
    offset_ref, keys, values, key_sum, value_sum, tile_sum = refs[-6:]
    out_refs = refs[-6 - ways : -6]
    rows = tiles_ref.shape[1]
    me = me_ref[0]
    keys[...] = qkv_ref[0, HEAD : 2 * HEAD].T
    values[...] = qkv_ref[0, 2 * HEAD :].T
    key_sum[...] = jnp.zeros(key_sum.shape, F32)
    value_sum[...] = jnp.zeros(value_sum.shape, F32)
    tile_sum[...] = jnp.zeros(tile_sum.shape, F32)
    for query_block in range(ways):
        query_rows = slice(query_block * rows, (query_block + 1) * rows)
        starts = [tile_start(me, place, query_block, ways, rows) for place in range(ways)]
        query = qkv_ref[0, :HEAD, query_rows]
        grad = grad_refs[query_block][0]
        total = total_ref[0, 0, :, query_rows]
        probs, weight_grads = [], []
        inner = jnp.zeros((1, rows), F32)
        for place in range(ways):
            key_rows = slice(place * rows, (place + 1) * rows)
            scores = dot_of(keys[key_rows], query, 1, 0) * (SCORE_SCALE * LOG2E)
            prob = jnp.exp2(scores + (tiles_ref[0, :, pl.ds(starts[place], rows)] - total))
            weight_grad = dot_of(values[key_rows], grad, 1, 0)
            inner = inner + jnp.sum(prob * weight_grad, axis=0, keepdims=True)
            value_sum[:, key_rows] += dot_of(grad, prob.astype(BF16), 1, 1)
            probs.append(prob)
            weight_grads.append(weight_grad)
        query_grad = jnp.zeros((HEAD, rows), F32)
        for place in range(ways):
            key_rows = slice(place * rows, (place + 1) * rows)
            score_grad = probs[place] * (weight_grads[place] - inner)
            tile_sum[:, pl.ds(starts[place], rows)] += score_grad
            score_low = score_grad.astype(BF16)
            key_sum[:, key_rows] += dot_of(query, score_low, 1, 1)
            query_grad = query_grad + dot_of(
                qkv_ref[0, HEAD : 2 * HEAD, key_rows], score_low, 1, 0
            )
        out_refs[query_block][0, :HEAD] = (query_grad * SCORE_SCALE).astype(BF16)
    for place in range(ways):
        key_rows = slice(place * rows, (place + 1) * rows)
        out_refs[place][0, HEAD : 2 * HEAD] = (key_sum[:, key_rows] * SCORE_SCALE).astype(BF16)
        out_refs[place][0, 2 * HEAD :] = value_sum[:, key_rows].astype(BF16)
    folded, half = tile_sum[...], rows // 2
    while half:
        folded = pltpu.roll(folded[:half], half, 1) + folded[half:]
        half //= 2
    offset_ref[0] = folded


def attend_back(me, qkv, grads, totals, tiles, span, head, earlier):
    seq_count, _, length = qkv.shape
    _, rows, columns = tiles.shape
    ways = length // rows
    results = pl.pallas_call(
        attend_back_kernel,
        grid=(seq_count,),
        out_shape=[jax.ShapeDtypeStruct((seq_count, 3 * HEAD, rows), BF16)] * ways
        + [jax.ShapeDtypeStruct((seq_count, 1, span), F32)],
        in_specs=[
            pl.BlockSpec(memory_space=pltpu.SMEM),
            pl.BlockSpec((1, 3 * HEAD, length), lambda i: (i, head, 0)),
        ]
        + [pl.BlockSpec((1, HEAD, rows), lambda i: (i, head, 0))] * ways
        + [
            pl.BlockSpec((1, 1, 1, length), lambda i: (i, head, 0, 0)),
            pl.BlockSpec((1, rows, columns), lambda i: (head, 0, 0)),
        ]
        + [pl.BlockSpec(memory_space=pl.ANY)] * len(earlier),
        out_specs=[pl.BlockSpec((1, 3 * HEAD, rows), lambda i: (i, 0, 0))] * ways
        + [pl.BlockSpec((1, 1, span), lambda i: (i, 0, 0))],
        scratch_shapes=[
            pltpu.VMEM((length, HEAD), BF16),
            pltpu.VMEM((length, HEAD), BF16),
            pltpu.VMEM((HEAD, length), F32),
            pltpu.VMEM((HEAD, length), F32),
            pltpu.VMEM((rows, span), F32),
        ],
        compiler_params=pltpu.CompilerParams(vmem_limit_bytes=VMEM_LIMIT),
        cost_estimate=kernel_cost(80),
        name="attend_back",
    )(me, qkv, *grads, totals, tiles, *earlier)
    return results[:ways], results[ways]


def column_kernel(normed_ref, columns_ref, *refs):
    ways = normed_ref.shape[1] // refs[0].shape[2]
    heads = columns_ref.shape[1] // refs[0].shape[1]
    grad_refs = refs[: heads * ways]
    out_ref, gain_ref = refs[-2:]
    rows = refs[0].shape[2]
    parts = []
    for head in range(heads):
        part = 0.0
        for seq in range(normed_ref.shape[0]):
            for r in range(ways):
                part += dot_of(
                    grad_refs[head * ways + r][seq],
                    normed_ref[seq, r * rows : (r + 1) * rows],
                    1,
                    0,
                )
        parts.append(part)
    total = jnp.concatenate(parts, axis=0).T
    out_ref[...] = total.astype(BF16)
    gain_ref[...] = jnp.sum(total * columns_ref[...].astype(F32), axis=1, keepdims=True)


def column_grads(normed, columns, grads, earlier):
    count = 2 + len(grads)
    return pl.pallas_call(
        column_kernel,
        out_shape=(
            jax.ShapeDtypeStruct(columns.shape, BF16),
            jax.ShapeDtypeStruct((columns.shape[0], 1), F32),
        ),
        in_specs=[pl.BlockSpec(memory_space=pltpu.VMEM)] * count
        + [pl.BlockSpec(memory_space=pl.ANY)] * len(earlier),
        out_specs=[pl.BlockSpec(memory_space=pltpu.VMEM)] * 2,
        compiler_params=pltpu.CompilerParams(vmem_limit_bytes=VMEM_LIMIT),
        cost_estimate=kernel_cost(5),
        name="column_grads",
    )(normed, columns, *grads, *earlier)


def token_grads(me, tokens, hidden_grad, gain, weights, first_block, moved, earlier):
    seq_count, rows, model_width = tokens.shape
    shards = weights.shape[0]
    own_rows = model_width // shards
    local_heads, ways = len(moved), len(moved[0])
    grads = [grad for blocks in moved for grad in blocks]
    block = pl.BlockSpec((1, rows, model_width), lambda i: (i, 0, 0))

    def kernel(me_ref, tokens_ref, hidden_grad_ref, gain_ref, *refs):
        weight_refs, grad_refs = refs[:3], refs[3 : 3 + len(grads)]
        out_ref, gathered = refs[-2:]
        for head in range(local_heads):
            for r in range(ways):
                place = lax.rem(me_ref[0] - r + ways, ways) * local_heads + head
                place = pl.multiple_of(place * HEAD, HEAD)
                for kind in range(3):
                    gathered[kind, pl.ds(place, HEAD)] = grad_refs[head * ways + r][
                        0, kind * HEAD : (kind + 1) * HEAD
                    ]
        normed_grad = 0.0
        for kind in range(3):
            weight = weight_refs[kind][...].reshape(model_width, model_width)
            normed_grad += dot_of(gathered[kind], weight, 0, 1)
        inputs = tokens_ref[0].astype(F32)
        scale = norm_scale(inputs)
        weighted = normed_grad * gain_ref[...]
        inner_sum = jnp.mean(weighted * inputs, axis=-1, keepdims=True)
        out_ref[0] = (
            hidden_grad_ref[0] + scale * weighted - inputs * (scale * scale * scale) * inner_sum
        )

    def weight_spec(place):
        return pl.BlockSpec((shards, own_rows, model_width), lambda i: (0, place, 0))

    weights, weight_specs = [weights] * 3, [weight_spec(first_block + kind) for kind in range(3)]
    if own_rows % 16:
        weights = [
            weights[0][:, (first_block + kind) * own_rows : (first_block + kind + 1) * own_rows]
            for kind in range(3)
        ]
        weight_specs = [weight_spec(0)] * 3
    return pl.pallas_call(
        kernel,
        grid=(seq_count,),
        out_shape=jax.ShapeDtypeStruct(tokens.shape, F32),
        in_specs=[
            pl.BlockSpec(memory_space=pltpu.SMEM),
            block,
            block,
            pl.BlockSpec((1, model_width), lambda i: (0, 0)),
        ]
        + weight_specs
        + [pl.BlockSpec((1,) + grads[0].shape[1:], lambda i: (i, 0, 0))] * len(grads)
        + [pl.BlockSpec(memory_space=pl.ANY)] * len(earlier),
        out_specs=block,
        scratch_shapes=[pltpu.VMEM((3, model_width, rows), BF16)],
        compiler_params=pltpu.CompilerParams(vmem_limit_bytes=VMEM_LIMIT),
        cost_estimate=kernel_cost(6),
        name="token_grads",
    )(me, tokens, hidden_grad, gain, *weights, *grads, *earlier)


def out_grads(places, contexts, grads, ways, shards):
    seq_count, model_width, rows = contexts.shape
    width, per_group = model_width // ways, shards // ways
    own_rows = model_width // shards

    def kernel(places_ref, contexts_ref, grads_ref, kept_ref, sent_ref):
        even = places_ref[1] % 2 == 0
        for r in range(ways):
            part = 0.0
            for seq in range(seq_count):
                part += dot_of(
                    contexts_ref[seq, r * width : (r + 1) * width], grads_ref[seq], 1, 0
                )
            pairs = part.reshape(per_group // 2, 2, own_rows, model_width)
            group = lax.rem(places_ref[0] - r + ways, ways)
            place = pl.ds(group * (per_group // 2), per_group // 2)
            kept_ref[place] = jnp.where(even, pairs[:, 0], pairs[:, 1]).astype(BF16)
            sent_ref[place] = jnp.where(even, pairs[:, 1], pairs[:, 0]).astype(BF16)

    return pl.pallas_call(
        kernel,
        out_shape=[jax.ShapeDtypeStruct((shards // 2, own_rows, model_width), BF16)] * 2,
        in_specs=[pl.BlockSpec(memory_space=pltpu.SMEM)]
        + [pl.BlockSpec(memory_space=pltpu.VMEM)] * 2,
        out_specs=[pl.BlockSpec(memory_space=pltpu.VMEM)] * 2,
        compiler_params=pltpu.CompilerParams(vmem_limit_bytes=VMEM_LIMIT),
        cost_estimate=kernel_cost(3),
        name="out_grads",
    )(places, contexts, grads)


def experts_kernel(*refs):
    weights_ref = refs[6]
    slots, plain, gates = [
        jnp.concatenate([refs[k][0], refs[k + 1][0]], axis=0) for k in (0, 2, 4)
    ]
    plain = plain.astype(F32)
    grads = (plain * gates).astype(BF16)
    shards, rows, model_width = weights_ref.shape
    units = rows // 2
    up = weights_ref[:, :units].reshape(shards * units, model_width)
    down = weights_ref[:, units:].reshape(shards * units, model_width)
    pre = dot_of(slots, up, 1, 1)
    normal_cdf = 0.5 * (1.0 + lax.erf(pre * ROOT_HALF))
    act = (pre * normal_cdf).astype(BF16)
    slope = normal_cdf + pre * jnp.exp(-0.5 * pre * pre) * DENSITY
    act_grad = dot_of(grads, down, 1, 1)
    pre_grad = (act_grad * slope).astype(BF16)
    returned = dot_of(act, down, 1, 0)
    back = dot_of(pre_grad, up, 1, 0)
    if len(refs) == 10:
        out_ref, back_ref, parts_ref = refs[7:]
        out_ref[0] = returned
        back_ref[0] = back
    else:
        out_ref, far_out_ref, back_ref, far_back_ref, gate_ref, far_gate_ref, parts_ref = refs[10:]
        half = slots.shape[0] // 2
        returned += refs[7][0]
        back += refs[8][0]
        gate_parts = jnp.sum(returned * plain, axis=1, keepdims=True)
        out_ref[0] = returned[:half].astype(BF16)
        far_out_ref[0] = returned[half:].astype(BF16)
        back_ref[0] = back[:half].astype(BF16)
        far_back_ref[0] = back[half:].astype(BF16)
        gate_ref[0] = gate_parts[:half]
        far_gate_ref[0] = gate_parts[half:]
    part_shape = (shards, units, model_width)
    parts_ref[:, :units] = dot_of(pre_grad, slots, 0, 0).astype(BF16).reshape(part_shape)
    parts_ref[:, units:] = dot_of(act, grads, 0, 0).astype(BF16).reshape(part_shape)


def experts(slots, grads, gates, weights, units, before):
    expert_count, rows, model_width = slots[0].shape
    shards = weights.shape[0]
    row_spec = pl.BlockSpec((1, rows, model_width), lambda e: (e, 0, 0))
    gate_spec = pl.BlockSpec((1, rows, 1), lambda e: (e, 0, 0))
    both_spec = pl.BlockSpec((1, 2 * rows, model_width), lambda e: (e, 0, 0))
    weight_block = (shards, 2 * units, model_width)
    place = expert_count if before else 0
    both = jax.ShapeDtypeStruct((expert_count, 2 * rows, model_width), F32)
    half = jax.ShapeDtypeStruct((expert_count, rows, model_width), BF16)
    gate = jax.ShapeDtypeStruct((expert_count, rows, 1), F32)
    parts = jax.ShapeDtypeStruct((shards, 4 * expert_count * units, model_width), BF16)
    parts_spec = pl.BlockSpec(weight_block, lambda e: (0, place + e, 0))
    return pl.pallas_call(
        experts_kernel,
        grid=(expert_count,),
        out_shape=[half] * 4 + [gate] * 2 + [parts] if before else [both] * 2 + [parts],
        in_specs=[row_spec] * 4
        + [gate_spec] * 2
        + [pl.BlockSpec(weight_block, lambda e: (0, e, 0))]
        + ([both_spec, both_spec, pl.BlockSpec(memory_space=pl.ANY)] if before else []),
        out_specs=(
            [row_spec] * 4 + [gate_spec] * 2 + [parts_spec]
            if before
            else [both_spec] * 2 + [parts_spec]
        ),
        input_output_aliases={9: 6} if before else {},
        compiler_params=pltpu.CompilerParams(vmem_limit_bytes=VMEM_LIMIT),
        cost_estimate=kernel_cost(9),
        name="experts",
    )(*slots, *grads, *gates, weights, *before)


def turned(values, axis_name, step):
    ways = lax.axis_size(axis_name)
    return lax.ppermute(values, axis_name, [((i + step) % ways, i) for i in range(ways)])


def following_kernel(*refs):
    pass


def following(values, *earlier):
    anywhere = pl.BlockSpec(memory_space=pl.ANY)
    return pl.pallas_call(
        following_kernel,
        out_shape=jax.ShapeDtypeStruct(values.shape, values.dtype),
        in_specs=[anywhere] * (1 + len(earlier)),
        out_specs=anywhere,
        input_output_aliases={0: 0},
        name="following",
    )(values, *earlier)


def flipped(values, axis_name, bit):
    ways = lax.axis_size(axis_name)
    return lax.ppermute(values, axis_name, [(i, i ^ (1 << bit)) for i in range(ways)])


def sum_everywhere(values, axis_names):
    for axis_name in axis_names:
        for bit in range(lax.axis_size(axis_name).bit_length() - 1):
            values = values + flipped(values, axis_name, bit)
    return values


def scattered_steps(values, axis_name, order, waits, summed=None):
    steps, left = [], sorted(order, reverse=True)
    place = jnp.full((1,), lax.axis_index(axis_name), jnp.int32)
    parts = values.reshape((2,) * len(order) + (-1,) + values.shape[1:])
    for bit in order:
        earlier = list(waits.get(bit, ()))
        if summed is not None and steps:
            earlier.append(summed)
            summed = following(summed, parts)
        if earlier:
            place = following(place, *earlier)
        mine = (place[0] >> bit) & 1
        axis = left.index(bit)
        left.remove(bit)
        kept = lax.dynamic_index_in_dim(parts, mine, axis, keepdims=False)
        sent = lax.dynamic_index_in_dim(parts, 1 - mine, axis, keepdims=False)
        received = flipped(sent, axis_name, bit)
        parts = (kept.astype(F32) + received.astype(F32)).astype(values.dtype)
        if summed is not None:
            summed = summed + flipped(summed, axis_name, bit)
        steps.append(parts)
    return steps if summed is None else (steps, summed)


def cyclic(values, me, ways, axis, direction):
    size = values.shape[axis] // ways
    return jnp.concatenate(
        [
            lax.dynamic_slice_in_dim(
                values, lax.rem(me + direction * r + ways, ways) * size, size, axis
            )
            for r in range(ways)
        ],
        axis=axis,
    )


def shards(
    tokens,
    routes,
    buckets,
    gain_attn,
    w_query,
    w_key,
    w_value,
    w_out,
    bias_table,
    gain_ff,
    router,
    expert_up,
    expert_down,
    out_grad,
):
    seq_count, block_rows, model_width = tokens.shape
    ways = lax.axis_size("seq")
    group = lax.axis_size("fsdp")
    me = lax.axis_index("seq")
    length = block_rows * ways
    capacity = block_rows * 9 // 16
    expert_count = router.shape[1]
    token_rows = seq_count * block_rows
    slot_rows = seq_count * capacity
    width = model_width // ways
    local_heads = width // HEAD
    places = jnp.full((1,), me, jnp.int32)

    others = [turned(tokens, "seq", r) for r in range(1, ways)]

    def columns_of(place):
        parts = [
            lax.dynamic_slice_in_dim(weight, place * width, width, 1).reshape(-1, local_heads, HEAD)
            for weight in (w_query, w_key, w_value)
        ]
        return jnp.stack(parts, axis=2).reshape(-1, 3 * width)

    own_columns = lax.all_gather(columns_of(me), "fsdp", axis=0, tiled=True)

    units = expert_up.shape[1]
    expert_rows = 2 * expert_count * units
    own_rows = w_out.shape[0]
    own_experts = jnp.stack([expert_up, expert_down], axis=1).reshape(expert_rows, model_width)
    own_weights = lax.all_gather(
        jnp.concatenate([own_experts, w_out, w_query, w_key, w_value]), "fsdp", axis=0
    )
    out_cyclic = cyclic(
        own_weights[:, expert_rows : expert_rows + own_rows].reshape(model_width, model_width),
        me, ways, 0, -1,
    )

    chosen = routes[:, :, 0]
    picked = (chosen[:, :, None] == jnp.arange(expert_count)[None, None, :]).astype(F32)
    earlier = jnp.cumsum(picked, axis=1) - picked
    slot_number = jnp.sum(earlier * picked, axis=-1).astype(jnp.int32)
    slot_index = chosen * capacity + slot_number
    dispatch = (
        slot_index[:, None, :] == jnp.arange(expert_count * capacity)[None, :, None]
    ).reshape(seq_count, expert_count, capacity, block_rows)
    dispatch_low = dispatch.astype(BF16)

    def to_slots(values):
        placed = jnp.einsum("nect,ntd->encd", dispatch_low, values, preferred_element_type=F32)
        return placed.astype(BF16).reshape(expert_count, slot_rows, model_width)

    def from_slots(values):
        return jnp.einsum(
            "nect,encd->ntd",
            dispatch_low,
            values.astype(BF16).reshape(expert_count, seq_count, capacity, model_width),
            preferred_element_type=F32,
        )

    grad_slots = to_slots(out_grad)
    far_grad_slots = flipped(grad_slots, "seq", 0)

    table_here = lax.dynamic_slice_in_dim(bias_table, me * local_heads, local_heads, 1)
    bucket_table = (buckets[:, None] == jnp.arange(bias_table.shape[0])[None, :]).astype(F32)
    reversed_buckets = jnp.pad(bucket_table[::-1], ((0, 1), (0, 0)))
    reversed_bias = jnp.einsum(
        "uk,kh->hu", reversed_buckets, table_here * LOG2E, precision=PRECISE
    )
    tiles = bias_tiles(reversed_bias[:, None, :], block_rows, length * 2 - block_rows)

    far_experts = flipped(
        following(
            own_experts, *others, own_columns, tiles
        ),
        "seq",
        1,
    )
    normed_all, qkv = project(
        [tokens] + others, own_columns, gain_attn[None]
    )
    contexts, totals = attend(places, qkv, tiles)
    far_weights = lax.all_gather(following(far_experts, contexts[0]), "fsdp", axis=0)
    context_t = jnp.concatenate(
        [contexts[0]] + [turned(contexts[r], "seq", -r) for r in range(1, ways)], axis=1
    )
    attn_branch = jnp.einsum("nct,cd->ntd", context_t, out_cyclic, preferred_element_type=F32)
    inputs = tokens.astype(F32)
    hidden = inputs + attn_branch
    second_scale = norm_scale(hidden)
    ffnorm = hidden * second_scale * gain_ff
    logits = jnp.einsum("std,de->ste", ffnorm, router, precision=PRECISE)
    route_probs = jax.nn.softmax(logits, axis=-1)
    gate_value = jnp.sum(route_probs * picked, axis=-1)

    slots = to_slots(ffnorm.astype(BF16))
    gate_slots = jnp.einsum(
        "nect->enc", jnp.where(dispatch, gate_value[:, None, None, :], 0.0)
    ).reshape(expert_count, slot_rows)
    far_slots = flipped(slots, "seq", 0)
    far_gate_slots = flipped(gate_slots, "seq", 0)
    given = (
        (slots, far_slots),
        (grad_slots, far_grad_slots),
        (gate_slots[..., None], far_gate_slots[..., None]),
    )
    before = experts(*given, own_weights, units, ())
    returned, far_returned, slot_back, far_back, gate_parts, far_gate_parts, parts = experts(
        *given, far_weights, units, before
    )
    expert_share = lax.psum_scatter(parts, "fsdp", scatter_dimension=0, tiled=True)[0]
    far_chunks = []
    for chunk in jnp.split(expert_share[expert_rows:], 2):
        far_chunks.append(flipped(following(chunk, *far_chunks[-1:]), "seq", 1))
    gate_grad_slots = gate_parts[..., 0] + flipped(far_gate_parts[..., 0], "seq", 0)
    slot_sum = slot_back.astype(F32) + flipped(far_back, "seq", 0).astype(F32)
    upstream = out_grad.astype(F32)
    gate_grad = jnp.sum(
        jnp.where(
            dispatch,
            gate_grad_slots.reshape(expert_count, seq_count, capacity).transpose(1, 0, 2)[..., None],
            0.0,
        ),
        axis=(1, 2),
    )
    logit_grad = gate_value[:, :, None] * (picked - route_probs) * gate_grad[:, :, None]
    ffnorm_grad = from_slots(slot_sum) + jnp.einsum(
        "ste,de->std", logit_grad, router, precision=PRECISE
    )
    router_grad = jnp.einsum("std,ste->de", ffnorm, logit_grad, precision=PRECISE)
    weighted = ffnorm_grad * gain_ff
    inner_sum = jnp.mean(weighted * hidden, axis=-1, keepdims=True)
    hidden_grad = (
        upstream + second_scale * weighted - hidden * (second_scale**3) * inner_sum
    )
    gain_ff_grad = jnp.sum(ffnorm_grad * hidden * second_scale, axis=(0, 1))
    branch_grad = hidden_grad.astype(BF16)
    context_grad = jnp.einsum(
        "cd,ntd->nct", out_cyclic, branch_grad, preferred_element_type=F32
    ).astype(BF16)
    context_grads = [context_grad[:, :width]] + [
        turned(context_grad[:, r * width : (r + 1) * width], "seq", r) for r in range(1, ways)
    ]
    group = lax.axis_size("fsdp")
    out_kept, out_sent = out_grads(
        jnp.stack([me, lax.axis_index("fsdp")]).astype(jnp.int32), context_t, branch_grad, ways, group
    )
    out_half = (out_kept.astype(F32) + flipped(out_sent, "fsdp", 0).astype(F32)).astype(BF16)
    bits = list(range(1, group.bit_length() - 1))
    out_steps = [out_half] + scattered_steps(out_half, "fsdp", bits, {})
    out_steps[-1] = out_steps[-1].reshape(-1, model_width)
    far_returned = flipped(following(far_returned, *context_grads[1:]), "seq", 0)
    returned_sum = returned.astype(F32) + far_returned.astype(F32)
    output = (hidden + gate_value[:, :, None] * from_slots(returned_sum)).astype(BF16)
    out_share = out_steps[-1]
    out_pair = out_share.astype(F32) + flipped(out_share, "seq", 0).astype(F32)
    out_pair = out_pair.astype(BF16)
    far_pair = flipped(out_pair, "seq", 1)
    out_sum = out_pair.astype(F32) + far_pair.astype(F32)

    head_grads, moved_grads, offset_grads = [], [], []
    for head in range(local_heads):
        earlier = out_steps[:1] if head else []
        if head > 1:
            earlier = earlier + moved_grads[head - 2][1:] + [far_returned]
        head_grad, offset_grad = attend_back(
            places, qkv, context_grads, totals, tiles, 2 * length, head, earlier
        )
        head_grads += head_grad
        moved_grads.append(
            [head_grad[0]] + [turned(head_grad[r], "seq", -r) for r in range(1, ways)]
        )
        offset_grads.append(jnp.sum(offset_grad, axis=0))
    column_grad, gain_attn_part = column_grads(
        normed_all, own_columns, head_grads, moved_grads[-2][1:] + out_steps[1:2]
    )
    gain_attn_part = gain_attn_part[:, 0] / gain_attn

    table_part = jnp.einsum(
        "uk,hu->kh", reversed_buckets, jnp.concatenate(offset_grads, axis=0), precision=PRECISE
    )
    table_full = lax.dynamic_update_slice_in_dim(
        jnp.zeros(bias_table.shape, F32), table_part, me * local_heads, 1
    )
    small = jnp.concatenate(
        [gain_attn_part, gain_ff_grad, router_grad.reshape(-1), table_full.reshape(-1)]
    )
    waits = {0: moved_grads[-1][1:] + [expert_share], 1: out_steps[-1:], 2: far_chunks[:1]}
    column_steps, small = scattered_steps(column_grad, "fsdp", [0] + bits, waits, small)
    column_share = column_steps[-1].reshape(-1, 3 * width)
    small = sum_everywhere(following(small, column_share), ("seq",))
    tokens_grad = token_grads(
        places, tokens, hidden_grad, gain_attn[None], own_weights, expert_rows // own_rows + 1,
        moved_grads, [],
    )

    gain_attn_sum = small[:model_width]
    gain_ff_sum = small[model_width : 2 * model_width]
    router_sum = small[2 * model_width : 2 * model_width + router.size].reshape(router.shape)
    table_sum = small[2 * model_width + router.size :].reshape(bias_table.shape)

    expert_sum = expert_share[:expert_rows].astype(F32) + jnp.concatenate(far_chunks).astype(F32)
    expert_sum = expert_sum.reshape(expert_count, 2, units, model_width)
    column_shares = jnp.concatenate(
        [column_share] + [turned(column_share, "seq", r) for r in range(1, ways)], axis=1
    )
    column_shares = cyclic(column_shares, ways - me, ways, 1, 1).astype(F32)
    column_shares = column_shares.reshape(-1, ways * local_heads, 3, HEAD)
    attn_sums = [column_shares[:, :, kind].reshape(-1, model_width) for kind in range(3)]
    return (
        output,
        tokens_grad,
        gain_attn_sum,
        attn_sums[0],
        attn_sums[1],
        attn_sums[2],
        out_sum,
        table_sum,
        gain_ff_sum,
        router_sum,
        expert_sum[:, 0],
        expert_sum[:, 1],
    )


def solution(mesh):
    in_specs = (
        P("fsdp", "seq", None),
        P("fsdp", "seq", None),
        P(),
        P(),
        P("fsdp", None),
        P("fsdp", None),
        P("fsdp", None),
        P("fsdp", None),
        P(),
        P(),
        P(),
        P(None, ("seq", "fsdp"), None),
        P(None, ("seq", "fsdp"), None),
        P("fsdp", "seq", None),
    )
    out_specs = (
        P("fsdp", "seq", None),
        P("fsdp", "seq", None),
        P(),
        P("fsdp", None),
        P("fsdp", None),
        P("fsdp", None),
        P("fsdp", None),
        P(),
        P(),
        P(),
        P(None, ("seq", "fsdp"), None),
        P(None, ("seq", "fsdp"), None),
    )
    return jax.shard_map(shards, mesh=mesh, in_specs=in_specs, out_specs=out_specs, check_vma=False)
```

```python
import jax
import jax.numpy as jnp
from jax import lax
from jax.experimental import pallas as pl
from jax.experimental.pallas import tpu as pltpu
from jax.sharding import PartitionSpec as P

HEAD = 64
EPSILON = 1e-06
PRECISE = lax.Precision.HIGHEST
ROOT_HALF = 0.7071067811865476
DENSITY = 0.3989422804014327
LOG2E = 1.4426950408889634
SCORE_SCALE = HEAD ** (-0.5)
VMEM_LIMIT = 56 * 1024 * 1024
BF16 = jnp.bfloat16
F32 = jnp.float32


def dot_of(left, right, left_dim, right_dim):
    return lax.dot_general(
        left, right, (((left_dim,), (right_dim,)), ((), ())), preferred_element_type=F32
    )


def kernel_cost(microseconds):
    return pl.CostEstimate(
        flops=int(microseconds * 8e7), bytes_accessed=int(microseconds * 3e5), transcendentals=0
    )


def norm_scale(values):
    return lax.rsqrt(jnp.mean(values * values, axis=-1, keepdims=True) + EPSILON)


def bias_tiles_kernel(reversed_ref, tiles_ref):
    rows = tiles_ref.shape[1]
    width = reversed_ref.shape[2]
    for head in range(tiles_ref.shape[0]):
        line = jnp.broadcast_to(reversed_ref[head], (rows, width))
        skewed = pltpu.roll(line, width - (rows - 1), 1, stride=1, stride_axis=0)
        tiles_ref[head] = skewed[:, : tiles_ref.shape[2]]


def bias_tiles(reversed_bias, rows, columns):
    heads = reversed_bias.shape[0]
    return pl.pallas_call(
        bias_tiles_kernel,
        out_shape=jax.ShapeDtypeStruct((heads, rows, columns), F32),
        in_specs=[pl.BlockSpec(memory_space=pltpu.VMEM)],
        out_specs=pl.BlockSpec(memory_space=pltpu.VMEM),
        compiler_params=pltpu.CompilerParams(vmem_limit_bytes=VMEM_LIMIT),
        cost_estimate=kernel_cost(4),
        name="bias_tiles",
    )(reversed_bias)


def tile_start(me, key_block, query_block, ways, rows):
    key_place = lax.rem(me + key_block, ways)
    query_place = lax.rem(me + query_block, ways)
    return pl.multiple_of((query_place - key_place + ways - 1) * rows, rows)


def project_kernel(*refs):
    columns_ref, gain_ref, normed_ref, qkv_ref = refs[-4:]
    rows = refs[0].shape[1]
    columns = columns_ref[...].T
    for r, block_ref in enumerate(refs[:-4]):
        values = block_ref[0].astype(F32)
        normed = (values * norm_scale(values) * gain_ref[...]).astype(BF16)
        normed_ref[0, r * rows : (r + 1) * rows] = normed
        qkv_ref[0, :, r * rows : (r + 1) * rows] = dot_of(columns, normed, 1, 1).astype(BF16)


def project(blocks, columns, gain):
    seq_count, rows, model_width = blocks[0].shape
    length = rows * len(blocks)
    triple = columns.shape[1]
    return pl.pallas_call(
        project_kernel,
        grid=(seq_count,),
        out_shape=(
            jax.ShapeDtypeStruct((seq_count, length, model_width), BF16),
            jax.ShapeDtypeStruct((seq_count, triple, length), BF16),
        ),
        in_specs=[pl.BlockSpec((1, rows, model_width), lambda i: (i, 0, 0))] * len(blocks)
        + [
            pl.BlockSpec((model_width, triple), lambda i: (0, 0)),
            pl.BlockSpec((1, model_width), lambda i: (0, 0)),
        ],
        out_specs=(
            pl.BlockSpec((1, length, model_width), lambda i: (i, 0, 0)),
            pl.BlockSpec((1, triple, length), lambda i: (i, 0, 0)),
        ),
        compiler_params=pltpu.CompilerParams(vmem_limit_bytes=VMEM_LIMIT),
        cost_estimate=kernel_cost(5),
        name="project",
    )(*blocks, columns, gain)


def attend_kernel(me_ref, qkv_ref, tiles_ref, *refs):
    context_refs, total_ref, keys = refs[:-2], refs[-2], refs[-1]
    heads, rows = tiles_ref.shape[0], tiles_ref.shape[1]
    ways = len(context_refs)
    me = me_ref[0]
    for head in range(heads):
        first = 3 * head * HEAD
        keys[head] = qkv_ref[0, first + HEAD : first + 2 * HEAD].T
    for query_block in range(ways):
        query_rows = slice(query_block * rows, (query_block + 1) * rows)
        starts = [tile_start(me, place, query_block, ways, rows) for place in range(ways)]
        for head in range(heads):
            first = 3 * head * HEAD
            query = qkv_ref[0, first : first + HEAD, query_rows]
            scores = [
                dot_of(keys[head, place * rows : (place + 1) * rows], query, 1, 0)
                * (SCORE_SCALE * LOG2E)
                + tiles_ref[head, :, pl.ds(starts[place], rows)]
                for place in range(ways)
            ]
            top = scores[0]
            for tile in scores[1:]:
                top = jnp.maximum(top, tile)
            top = jnp.max(top, axis=0, keepdims=True)
            total = jnp.zeros((1, rows), F32)
            context = jnp.zeros((HEAD, rows), F32)
            for place in range(ways):
                value = qkv_ref[
                    0, first + 2 * HEAD : first + 3 * HEAD, place * rows : (place + 1) * rows
                ]
                shifted = jnp.exp2(scores[place] - top)
                total = total + jnp.sum(shifted, axis=0, keepdims=True)
                context = context + dot_of(value, shifted.astype(BF16), 1, 0)
            context_refs[query_block][0, head * HEAD : (head + 1) * HEAD] = (
                context / total
            ).astype(BF16)
            total_ref[0, head, :, query_rows] = top + jnp.log2(total)


def attend(me, qkv, tiles):
    seq_count, triple, length = qkv.shape
    heads, rows, columns = tiles.shape
    width, ways = triple // 3, length // rows
    results = pl.pallas_call(
        attend_kernel,
        grid=(seq_count,),
        out_shape=[jax.ShapeDtypeStruct((seq_count, width, rows), BF16)] * ways
        + [jax.ShapeDtypeStruct((seq_count, heads, 1, length), F32)],
        in_specs=[
            pl.BlockSpec(memory_space=pltpu.SMEM),
            pl.BlockSpec((1, triple, length), lambda i: (i, 0, 0)),
            pl.BlockSpec((heads, rows, columns), lambda i: (0, 0, 0)),
        ],
        out_specs=[pl.BlockSpec((1, width, rows), lambda i: (i, 0, 0))] * ways
        + [pl.BlockSpec((1, heads, 1, length), lambda i: (i, 0, 0, 0))],
        scratch_shapes=[pltpu.VMEM((heads, length, HEAD), BF16)],
        compiler_params=pltpu.CompilerParams(vmem_limit_bytes=VMEM_LIMIT),
        cost_estimate=kernel_cost(11),
        name="attend",
    )(me, qkv, tiles)
    return results[:ways], results[ways]


def attend_back_kernel(me_ref, qkv_ref, *refs):
    ways = qkv_ref.shape[2] // refs[0].shape[2]
    grad_refs = refs[:ways]
    total_ref, tiles_ref = refs[ways : ways + 2]
    offset_ref, keys, values, key_sum, value_sum, tile_sum = refs[-6:]
    out_refs = refs[-6 - ways : -6]
    rows = tiles_ref.shape[1]
    me = me_ref[0]
    keys[...] = qkv_ref[0, HEAD : 2 * HEAD].T
    values[...] = qkv_ref[0, 2 * HEAD :].T
    key_sum[...] = jnp.zeros(key_sum.shape, F32)
    value_sum[...] = jnp.zeros(value_sum.shape, F32)
    tile_sum[...] = jnp.zeros(tile_sum.shape, F32)
    for query_block in range(ways):
        query_rows = slice(query_block * rows, (query_block + 1) * rows)
        starts = [tile_start(me, place, query_block, ways, rows) for place in range(ways)]
        query = qkv_ref[0, :HEAD, query_rows]
        grad = grad_refs[query_block][0]
        total = total_ref[0, 0, :, query_rows]
        probs, weight_grads = [], []
        inner = jnp.zeros((1, rows), F32)
        for place in range(ways):
            key_rows = slice(place * rows, (place + 1) * rows)
            scores = dot_of(keys[key_rows], query, 1, 0) * (SCORE_SCALE * LOG2E)
            prob = jnp.exp2(scores + (tiles_ref[0, :, pl.ds(starts[place], rows)] - total))
            weight_grad = dot_of(values[key_rows], grad, 1, 0)
            inner = inner + jnp.sum(prob * weight_grad, axis=0, keepdims=True)
            value_sum[:, key_rows] += dot_of(grad, prob.astype(BF16), 1, 1)
            probs.append(prob)
            weight_grads.append(weight_grad)
        query_grad = jnp.zeros((HEAD, rows), F32)
        for place in range(ways):
            key_rows = slice(place * rows, (place + 1) * rows)
            score_grad = probs[place] * (weight_grads[place] - inner)
            tile_sum[:, pl.ds(starts[place], rows)] += score_grad
            score_low = score_grad.astype(BF16)
            key_sum[:, key_rows] += dot_of(query, score_low, 1, 1)
            query_grad = query_grad + dot_of(
                qkv_ref[0, HEAD : 2 * HEAD, key_rows], score_low, 1, 0
            )
        out_refs[query_block][0, :HEAD] = (query_grad * SCORE_SCALE).astype(BF16)
    for place in range(ways):
        key_rows = slice(place * rows, (place + 1) * rows)
        out_refs[place][0, HEAD : 2 * HEAD] = (key_sum[:, key_rows] * SCORE_SCALE).astype(BF16)
        out_refs[place][0, 2 * HEAD :] = value_sum[:, key_rows].astype(BF16)
    folded, half = tile_sum[...], rows // 2
    while half:
        folded = pltpu.roll(folded[:half], half, 1) + folded[half:]
        half //= 2
    offset_ref[0] = folded


def attend_back(me, qkv, grads, totals, tiles, span, head, earlier):
    seq_count, _, length = qkv.shape
    _, rows, columns = tiles.shape
    ways = length // rows
    results = pl.pallas_call(
        attend_back_kernel,
        grid=(seq_count,),
        out_shape=[jax.ShapeDtypeStruct((seq_count, 3 * HEAD, rows), BF16)] * ways
        + [jax.ShapeDtypeStruct((seq_count, 1, span), F32)],
        in_specs=[
            pl.BlockSpec(memory_space=pltpu.SMEM),
            pl.BlockSpec((1, 3 * HEAD, length), lambda i: (i, head, 0)),
        ]
        + [pl.BlockSpec((1, HEAD, rows), lambda i: (i, head, 0))] * ways
        + [
            pl.BlockSpec((1, 1, 1, length), lambda i: (i, head, 0, 0)),
            pl.BlockSpec((1, rows, columns), lambda i: (head, 0, 0)),
        ]
        + [pl.BlockSpec(memory_space=pl.ANY)] * len(earlier),
        out_specs=[pl.BlockSpec((1, 3 * HEAD, rows), lambda i: (i, 0, 0))] * ways
        + [pl.BlockSpec((1, 1, span), lambda i: (i, 0, 0))],
        scratch_shapes=[
            pltpu.VMEM((length, HEAD), BF16),
            pltpu.VMEM((length, HEAD), BF16),
            pltpu.VMEM((HEAD, length), F32),
            pltpu.VMEM((HEAD, length), F32),
            pltpu.VMEM((rows, span), F32),
        ],
        compiler_params=pltpu.CompilerParams(vmem_limit_bytes=VMEM_LIMIT),
        cost_estimate=kernel_cost(80),
        name="attend_back",
    )(me, qkv, *grads, totals, tiles, *earlier)
    return results[:ways], results[ways]


def column_kernel(normed_ref, columns_ref, *refs):
    ways = normed_ref.shape[1] // refs[0].shape[2]
    heads = columns_ref.shape[1] // refs[0].shape[1]
    grad_refs = refs[: heads * ways]
    out_ref, gain_ref = refs[-2:]
    rows = refs[0].shape[2]
    parts = []
    for head in range(heads):
        part = 0.0
        for seq in range(normed_ref.shape[0]):
            for r in range(ways):
                part += dot_of(
                    grad_refs[head * ways + r][seq],
                    normed_ref[seq, r * rows : (r + 1) * rows],
                    1,
                    0,
                )
        parts.append(part)
    total = jnp.concatenate(parts, axis=0).T
    out_ref[...] = total.astype(BF16)
    gain_ref[...] = jnp.sum(total * columns_ref[...].astype(F32), axis=1, keepdims=True)


def column_grads(normed, columns, grads, earlier):
    count = 2 + len(grads)
    return pl.pallas_call(
        column_kernel,
        out_shape=(
            jax.ShapeDtypeStruct(columns.shape, BF16),
            jax.ShapeDtypeStruct((columns.shape[0], 1), F32),
        ),
        in_specs=[pl.BlockSpec(memory_space=pltpu.VMEM)] * count
        + [pl.BlockSpec(memory_space=pl.ANY)] * len(earlier),
        out_specs=[pl.BlockSpec(memory_space=pltpu.VMEM)] * 2,
        compiler_params=pltpu.CompilerParams(vmem_limit_bytes=VMEM_LIMIT),
        cost_estimate=kernel_cost(5),
        name="column_grads",
    )(normed, columns, *grads, *earlier)


def token_grads(me, tokens, hidden_grad, gain, weights, first_block, moved, earlier):
    seq_count, rows, model_width = tokens.shape
    shards = weights.shape[0]
    own_rows = model_width // shards
    local_heads, ways = len(moved), len(moved[0])
    grads = [grad for blocks in moved for grad in blocks]
    block = pl.BlockSpec((1, rows, model_width), lambda i: (i, 0, 0))

    def kernel(me_ref, tokens_ref, hidden_grad_ref, gain_ref, *refs):
        weight_refs, grad_refs = refs[:3], refs[3 : 3 + len(grads)]
        out_ref, gathered = refs[-2:]
        for head in range(local_heads):
            for r in range(ways):
                place = lax.rem(me_ref[0] - r + ways, ways) * local_heads + head
                place = pl.multiple_of(place * HEAD, HEAD)
                for kind in range(3):
                    gathered[kind, pl.ds(place, HEAD)] = grad_refs[head * ways + r][
                        0, kind * HEAD : (kind + 1) * HEAD
                    ]
        normed_grad = 0.0
        for kind in range(3):
            weight = weight_refs[kind][...].reshape(model_width, model_width)
            normed_grad += dot_of(gathered[kind], weight, 0, 1)
        inputs = tokens_ref[0].astype(F32)
        scale = norm_scale(inputs)
        weighted = normed_grad * gain_ref[...]
        inner_sum = jnp.mean(weighted * inputs, axis=-1, keepdims=True)
        out_ref[0] = (
            hidden_grad_ref[0] + scale * weighted - inputs * (scale * scale * scale) * inner_sum
        )

    def weight_spec(place):
        return pl.BlockSpec((shards, own_rows, model_width), lambda i: (0, place, 0))

    weights, weight_specs = [weights] * 3, [weight_spec(first_block + kind) for kind in range(3)]
    if own_rows % 16:
        weights = [
            weights[0][:, (first_block + kind) * own_rows : (first_block + kind + 1) * own_rows]
            for kind in range(3)
        ]
        weight_specs = [weight_spec(0)] * 3
    return pl.pallas_call(
        kernel,
        grid=(seq_count,),
        out_shape=jax.ShapeDtypeStruct(tokens.shape, F32),
        in_specs=[
            pl.BlockSpec(memory_space=pltpu.SMEM),
            block,
            block,
            pl.BlockSpec((1, model_width), lambda i: (0, 0)),
        ]
        + weight_specs
        + [pl.BlockSpec((1,) + grads[0].shape[1:], lambda i: (i, 0, 0))] * len(grads)
        + [pl.BlockSpec(memory_space=pl.ANY)] * len(earlier),
        out_specs=block,
        scratch_shapes=[pltpu.VMEM((3, model_width, rows), BF16)],
        compiler_params=pltpu.CompilerParams(vmem_limit_bytes=VMEM_LIMIT),
        cost_estimate=kernel_cost(6),
        name="token_grads",
    )(me, tokens, hidden_grad, gain, *weights, *grads, *earlier)


def out_grads(places, contexts, grads, ways, shards, earlier):
    seq_count, model_width, rows = contexts.shape
    width, per_group = model_width // ways, shards // ways
    own_rows = model_width // shards

    def kernel(places_ref, contexts_ref, grads_ref, *refs):
        kept_ref, sent_ref = refs[-2:]
        even = places_ref[1] % 2 == 0
        for r in range(ways):
            part = 0.0
            for seq in range(seq_count):
                part += dot_of(
                    contexts_ref[seq, r * width : (r + 1) * width], grads_ref[seq], 1, 0
                )
            pairs = part.reshape(per_group // 2, 2, own_rows, model_width)
            group = lax.rem(places_ref[0] - r + ways, ways)
            place = pl.ds(group * (per_group // 2), per_group // 2)
            kept_ref[place] = jnp.where(even, pairs[:, 0], pairs[:, 1]).astype(BF16)
            sent_ref[place] = jnp.where(even, pairs[:, 1], pairs[:, 0]).astype(BF16)

    return pl.pallas_call(
        kernel,
        out_shape=[jax.ShapeDtypeStruct((shards // 2, own_rows, model_width), BF16)] * 2,
        in_specs=[pl.BlockSpec(memory_space=pltpu.SMEM)]
        + [pl.BlockSpec(memory_space=pltpu.VMEM)] * 2
        + [pl.BlockSpec(memory_space=pl.ANY)] * len(earlier),
        out_specs=[pl.BlockSpec(memory_space=pltpu.VMEM)] * 2,
        compiler_params=pltpu.CompilerParams(vmem_limit_bytes=VMEM_LIMIT),
        cost_estimate=kernel_cost(3),
        name="out_grads",
    )(places, contexts, grads, *earlier)


def experts_kernel(*refs):
    weights_ref = refs[6]
    slots, plain, gates = [
        jnp.concatenate([refs[k][0], refs[k + 1][0]], axis=0) for k in (0, 2, 4)
    ]
    plain = plain.astype(F32)
    grads = (plain * gates).astype(BF16)
    shards, rows, model_width = weights_ref.shape
    units = rows // 2
    up = weights_ref[:, :units].reshape(shards * units, model_width)
    down = weights_ref[:, units:].reshape(shards * units, model_width)
    pre = dot_of(slots, up, 1, 1)
    normal_cdf = 0.5 * (1.0 + lax.erf(pre * ROOT_HALF))
    act = (pre * normal_cdf).astype(BF16)
    slope = normal_cdf + pre * jnp.exp(-0.5 * pre * pre) * DENSITY
    act_grad = dot_of(grads, down, 1, 1)
    pre_grad = (act_grad * slope).astype(BF16)
    returned = dot_of(act, down, 1, 0)
    back = dot_of(pre_grad, up, 1, 0)
    if len(refs) == 10:
        out_ref, back_ref, parts_ref = refs[7:]
        out_ref[0] = returned
        back_ref[0] = back
    else:
        out_ref, far_out_ref, back_ref, far_back_ref, gate_ref, far_gate_ref, parts_ref = refs[10:]
        half = slots.shape[0] // 2
        returned += refs[7][0]
        back += refs[8][0]
        gate_parts = jnp.sum(returned * plain, axis=1, keepdims=True)
        out_ref[0] = returned[:half].astype(BF16)
        far_out_ref[0] = returned[half:].astype(BF16)
        back_ref[0] = back[:half].astype(BF16)
        far_back_ref[0] = back[half:].astype(BF16)
        gate_ref[0] = gate_parts[:half]
        far_gate_ref[0] = gate_parts[half:]
    part_shape = (shards, units, model_width)
    parts_ref[:, :units] = dot_of(pre_grad, slots, 0, 0).astype(BF16).reshape(part_shape)
    parts_ref[:, units:] = dot_of(act, grads, 0, 0).astype(BF16).reshape(part_shape)


def experts(slots, grads, gates, weights, units, before):
    expert_count, rows, model_width = slots[0].shape
    shards = weights.shape[0]
    row_spec = pl.BlockSpec((1, rows, model_width), lambda e: (e, 0, 0))
    gate_spec = pl.BlockSpec((1, rows, 1), lambda e: (e, 0, 0))
    both_spec = pl.BlockSpec((1, 2 * rows, model_width), lambda e: (e, 0, 0))
    weight_block = (shards, 2 * units, model_width)
    place = expert_count if before else 0
    both = jax.ShapeDtypeStruct((expert_count, 2 * rows, model_width), F32)
    half = jax.ShapeDtypeStruct((expert_count, rows, model_width), BF16)
    gate = jax.ShapeDtypeStruct((expert_count, rows, 1), F32)
    parts = jax.ShapeDtypeStruct((shards, 4 * expert_count * units, model_width), BF16)
    parts_spec = pl.BlockSpec(weight_block, lambda e: (0, place + e, 0))
    return pl.pallas_call(
        experts_kernel,
        grid=(expert_count,),
        out_shape=[half] * 4 + [gate] * 2 + [parts] if before else [both] * 2 + [parts],
        in_specs=[row_spec] * 4
        + [gate_spec] * 2
        + [pl.BlockSpec(weight_block, lambda e: (0, e, 0))]
        + ([both_spec, both_spec, pl.BlockSpec(memory_space=pl.ANY)] if before else []),
        out_specs=(
            [row_spec] * 4 + [gate_spec] * 2 + [parts_spec]
            if before
            else [both_spec] * 2 + [parts_spec]
        ),
        input_output_aliases={9: 6} if before else {},
        compiler_params=pltpu.CompilerParams(vmem_limit_bytes=VMEM_LIMIT),
        cost_estimate=kernel_cost(9),
        name="experts",
    )(*slots, *grads, *gates, weights, *before)


def turned(values, axis_name, step):
    ways = lax.axis_size(axis_name)
    return lax.ppermute(values, axis_name, [((i + step) % ways, i) for i in range(ways)])


def following_kernel(*refs):
    pass


def following(values, *earlier):
    anywhere = pl.BlockSpec(memory_space=pl.ANY)
    return pl.pallas_call(
        following_kernel,
        out_shape=jax.ShapeDtypeStruct(values.shape, values.dtype),
        in_specs=[anywhere] * (1 + len(earlier)),
        out_specs=anywhere,
        input_output_aliases={0: 0},
        cost_estimate=kernel_cost(1),
        name="following",
    )(values, *earlier)


def flipped(values, axis_name, bit):
    ways = lax.axis_size(axis_name)
    return lax.ppermute(values, axis_name, [(i, i ^ (1 << bit)) for i in range(ways)])


def sum_everywhere(values, axis_names):
    for axis_name in axis_names:
        for bit in range(lax.axis_size(axis_name).bit_length() - 1):
            values = values + flipped(values, axis_name, bit)
    return values


def scattered_steps(values, axis_name, order, waits):
    steps, left = [], sorted(order, reverse=True)
    place = jnp.full((1,), lax.axis_index(axis_name), jnp.int32)
    parts = values.reshape((2,) * len(order) + (-1,) + values.shape[1:])
    for bit in order:
        if bit in waits:
            place = following(place, *waits[bit])
        mine = (place[0] >> bit) & 1
        axis = left.index(bit)
        left.remove(bit)
        kept = lax.dynamic_index_in_dim(parts, mine, axis, keepdims=False)
        sent = lax.dynamic_index_in_dim(parts, 1 - mine, axis, keepdims=False)
        received = flipped(sent, axis_name, bit)
        parts = (kept.astype(F32) + received.astype(F32)).astype(values.dtype)
        steps.append(parts)
    return steps


def cyclic(values, me, ways, axis, direction):
    size = values.shape[axis] // ways
    return jnp.concatenate(
        [
            lax.dynamic_slice_in_dim(
                values, lax.rem(me + direction * r + ways, ways) * size, size, axis
            )
            for r in range(ways)
        ],
        axis=axis,
    )


def shards(
    tokens,
    routes,
    buckets,
    gain_attn,
    w_query,
    w_key,
    w_value,
    w_out,
    bias_table,
    gain_ff,
    router,
    expert_up,
    expert_down,
    out_grad,
):
    seq_count, block_rows, model_width = tokens.shape
    ways = lax.axis_size("seq")
    group = lax.axis_size("fsdp")
    me = lax.axis_index("seq")
    length = block_rows * ways
    capacity = block_rows * 9 // 16
    expert_count = router.shape[1]
    token_rows = seq_count * block_rows
    slot_rows = seq_count * capacity
    width = model_width // ways
    local_heads = width // HEAD
    places = jnp.full((1,), me, jnp.int32)

    others = [turned(tokens, "seq", r) for r in range(1, ways)]

    def columns_of(place):
        parts = [
            lax.dynamic_slice_in_dim(weight, place * width, width, 1).reshape(-1, local_heads, HEAD)
            for weight in (w_query, w_key, w_value)
        ]
        return jnp.stack(parts, axis=2).reshape(-1, 3 * width)

    own_columns = lax.all_gather(columns_of(me), "fsdp", axis=0, tiled=True)

    units = expert_up.shape[1]
    expert_rows = 2 * expert_count * units
    own_rows = w_out.shape[0]
    own_experts = jnp.stack([expert_up, expert_down], axis=1).reshape(expert_rows, model_width)
    own_weights = lax.all_gather(
        jnp.concatenate([own_experts, w_out, w_query, w_key, w_value]), "fsdp", axis=0
    )
    out_cyclic = cyclic(
        own_weights[:, expert_rows : expert_rows + own_rows].reshape(model_width, model_width),
        me, ways, 0, -1,
    )

    chosen = routes[:, :, 0]
    picked = (chosen[:, :, None] == jnp.arange(expert_count)[None, None, :]).astype(F32)
    earlier = jnp.cumsum(picked, axis=1) - picked
    slot_number = jnp.sum(earlier * picked, axis=-1).astype(jnp.int32)
    slot_index = chosen * capacity + slot_number
    dispatch = (
        slot_index[:, None, :] == jnp.arange(expert_count * capacity)[None, :, None]
    ).reshape(seq_count, expert_count, capacity, block_rows)
    dispatch_low = dispatch.astype(BF16)

    def to_slots(values):
        placed = jnp.einsum("nect,ntd->encd", dispatch_low, values, preferred_element_type=F32)
        return placed.astype(BF16).reshape(expert_count, slot_rows, model_width)

    def from_slots(values):
        return jnp.einsum(
            "nect,encd->ntd",
            dispatch_low,
            values.astype(BF16).reshape(expert_count, seq_count, capacity, model_width),
            preferred_element_type=F32,
        )

    grad_slots = to_slots(out_grad)
    far_grad_slots = flipped(grad_slots, "seq", 0)

    table_here = lax.dynamic_slice_in_dim(bias_table, me * local_heads, local_heads, 1)
    bucket_table = (buckets[:, None] == jnp.arange(bias_table.shape[0])[None, :]).astype(F32)
    reversed_buckets = jnp.pad(bucket_table[::-1], ((0, 1), (0, 0)))
    reversed_bias = jnp.einsum(
        "uk,kh->hu", reversed_buckets, table_here * LOG2E, precision=PRECISE
    )
    tiles = bias_tiles(reversed_bias[:, None, :], block_rows, length * 2 - block_rows)

    far_experts = flipped(
        following(
            own_experts, *others, own_columns, tiles
        ),
        "seq",
        1,
    )
    normed_all, qkv = project(
        [tokens] + others, own_columns, gain_attn[None]
    )
    contexts, totals = attend(places, qkv, tiles)
    far_weights = lax.all_gather(following(far_experts, contexts[0]), "fsdp", axis=0)
    context_t = jnp.concatenate(
        [contexts[0]] + [turned(contexts[r], "seq", -r) for r in range(1, ways)], axis=1
    )
    attn_branch = jnp.einsum("nct,cd->ntd", context_t, out_cyclic, preferred_element_type=F32)
    inputs = tokens.astype(F32)
    hidden = inputs + attn_branch
    second_scale = norm_scale(hidden)
    ffnorm = hidden * second_scale * gain_ff
    logits = jnp.einsum("std,de->ste", ffnorm, router, precision=PRECISE)
    route_probs = jax.nn.softmax(logits, axis=-1)
    gate_value = jnp.sum(route_probs * picked, axis=-1)

    slots = to_slots(ffnorm.astype(BF16))
    gate_slots = jnp.einsum(
        "nect->enc", jnp.where(dispatch, gate_value[:, None, None, :], 0.0)
    ).reshape(expert_count, slot_rows)
    far_slots = flipped(slots, "seq", 0)
    far_gate_slots = flipped(gate_slots, "seq", 0)
    given = (
        (slots, far_slots),
        (grad_slots, far_grad_slots),
        (gate_slots[..., None], far_gate_slots[..., None]),
    )
    before = experts(*given, own_weights, units, ())
    returned, far_returned, slot_back, far_back, gate_parts, far_gate_parts, parts = experts(
        *given, far_weights, units, before
    )
    expert_share = lax.psum_scatter(parts, "fsdp", scatter_dimension=0, tiled=True)[0]
    moved_share = flipped(expert_share[expert_rows:], "seq", 1)
    gate_grad_slots = gate_parts[..., 0] + flipped(far_gate_parts[..., 0], "seq", 0)
    slot_sum = slot_back.astype(F32) + flipped(far_back, "seq", 0).astype(F32)
    upstream = out_grad.astype(F32)
    gate_grad = jnp.sum(
        jnp.where(
            dispatch,
            gate_grad_slots.reshape(expert_count, seq_count, capacity).transpose(1, 0, 2)[..., None],
            0.0,
        ),
        axis=(1, 2),
    )
    logit_grad = gate_value[:, :, None] * (picked - route_probs) * gate_grad[:, :, None]
    ffnorm_grad = from_slots(slot_sum) + jnp.einsum(
        "ste,de->std", logit_grad, router, precision=PRECISE
    )
    router_grad = jnp.einsum("std,ste->de", ffnorm, logit_grad, precision=PRECISE)
    weighted = ffnorm_grad * gain_ff
    inner_sum = jnp.mean(weighted * hidden, axis=-1, keepdims=True)
    hidden_grad = (
        upstream + second_scale * weighted - hidden * (second_scale**3) * inner_sum
    )
    gain_ff_grad = jnp.sum(ffnorm_grad * hidden * second_scale, axis=(0, 1))
    branch_grad = hidden_grad.astype(BF16)
    context_grad = jnp.einsum(
        "cd,ntd->nct", out_cyclic, branch_grad, preferred_element_type=F32
    ).astype(BF16)
    context_grads = [context_grad[:, :width]] + [
        turned(context_grad[:, r * width : (r + 1) * width], "seq", r) for r in range(1, ways)
    ]
    group = lax.axis_size("fsdp")
    out_kept, out_sent = out_grads(
        jnp.stack([me, lax.axis_index("fsdp")]).astype(jnp.int32), context_t, branch_grad, ways, group,
        [],
    )
    out_half = (out_kept.astype(F32) + flipped(out_sent, "fsdp", 0).astype(F32)).astype(BF16)
    bits = list(range(1, group.bit_length() - 1))
    out_steps = [out_half] + scattered_steps(out_half, "fsdp", bits, {})
    out_steps[-1] = out_steps[-1].reshape(-1, model_width)
    far_returned = flipped(following(far_returned, *context_grads[1:]), "seq", 0)
    returned_sum = returned.astype(F32) + far_returned.astype(F32)
    output = (hidden + gate_value[:, :, None] * from_slots(returned_sum)).astype(BF16)
    out_share = out_steps[-1]
    out_pair = out_share.astype(F32) + flipped(out_share, "seq", 0).astype(F32)
    out_pair = out_pair.astype(BF16)
    far_pair = flipped(out_pair, "seq", 1)
    out_sum = out_pair.astype(F32) + far_pair.astype(F32)

    head_grads, moved_grads, offset_grads = [], [], []
    for head in range(local_heads):
        earlier = out_steps[head : head + 1] if head else []
        if head > 1:
            earlier = earlier + moved_grads[head - 2][1:] + [far_returned]
        head_grad, offset_grad = attend_back(
            places, qkv, context_grads, totals, tiles, 2 * length, head, earlier
        )
        head_grads += head_grad
        moved_grads.append(
            [head_grad[0]] + [turned(head_grad[r], "seq", -r) for r in range(1, ways)]
        )
        offset_grads.append(jnp.sum(offset_grad, axis=0))
    column_grad, gain_attn_part = column_grads(
        normed_all, own_columns, head_grads, moved_grads[-2][1:] + [out_pair]
    )
    gain_attn_part = gain_attn_part[:, 0] / gain_attn
    column_steps = scattered_steps(
        column_grad, "fsdp", [0] + bits, {}
    )
    column_share = column_steps[-1].reshape(-1, 3 * width)
    tokens_grad = token_grads(
        places, tokens, hidden_grad, gain_attn[None], own_weights, expert_rows // own_rows + 1,
        moved_grads, [column_grad],
    )

    table_part = jnp.einsum(
        "uk,hu->kh", reversed_buckets, jnp.concatenate(offset_grads, axis=0), precision=PRECISE
    )
    table_full = lax.dynamic_update_slice_in_dim(
        jnp.zeros(bias_table.shape, F32), table_part, me * local_heads, 1
    )
    small = jnp.concatenate(
        [gain_attn_part, gain_ff_grad, router_grad.reshape(-1), table_full.reshape(-1)]
    )
    small = sum_everywhere(small, ("fsdp",))
    small = sum_everywhere(following(small, moved_share), ("seq",))
    column_share = following(column_share, moved_share, tokens_grad)
    gain_attn_sum = small[:model_width]
    gain_ff_sum = small[model_width : 2 * model_width]
    router_sum = small[2 * model_width : 2 * model_width + router.size].reshape(router.shape)
    table_sum = small[2 * model_width + router.size :].reshape(bias_table.shape)

    expert_sum = expert_share[:expert_rows].astype(F32) + moved_share.astype(F32)
    expert_sum = expert_sum.reshape(expert_count, 2, units, model_width)
    column_shares = jnp.concatenate(
        [column_share] + [turned(column_share, "seq", r) for r in range(1, ways)], axis=1
    )
    column_shares = cyclic(column_shares, ways - me, ways, 1, 1).astype(F32)
    column_shares = column_shares.reshape(-1, ways * local_heads, 3, HEAD)
    attn_sums = [column_shares[:, :, kind].reshape(-1, model_width) for kind in range(3)]
    return (
        output,
        tokens_grad,
        gain_attn_sum,
        attn_sums[0],
        attn_sums[1],
        attn_sums[2],
        out_sum,
        table_sum,
        gain_ff_sum,
        router_sum,
        expert_sum[:, 0],
        expert_sum[:, 1],
    )


def solution(mesh):
    in_specs = (
        P("fsdp", "seq", None),
        P("fsdp", "seq", None),
        P(),
        P(),
        P("fsdp", None),
        P("fsdp", None),
        P("fsdp", None),
        P("fsdp", None),
        P(),
        P(),
        P(),
        P(None, ("seq", "fsdp"), None),
        P(None, ("seq", "fsdp"), None),
        P("fsdp", "seq", None),
    )
    out_specs = (
        P("fsdp", "seq", None),
        P("fsdp", "seq", None),
        P(),
        P("fsdp", None),
        P("fsdp", None),
        P("fsdp", None),
        P("fsdp", None),
        P(),
        P(),
        P(),
        P(None, ("seq", "fsdp"), None),
        P(None, ("seq", "fsdp"), None),
    )
    return jax.shard_map(shards, mesh=mesh, in_specs=in_specs, out_specs=out_specs, check_vma=False)
```

```python
import jax
import jax.numpy as jnp
from jax import lax
from jax.experimental import pallas as pl
from jax.experimental.pallas import tpu as pltpu
from jax.sharding import PartitionSpec as P

HEAD = 64
EPSILON = 1e-06
PRECISE = lax.Precision.HIGHEST
ROOT_HALF = 0.7071067811865476
DENSITY = 0.3989422804014327
LOG2E = 1.4426950408889634
SCORE_SCALE = HEAD ** (-0.5)
VMEM_LIMIT = 56 * 1024 * 1024
BF16 = jnp.bfloat16
F32 = jnp.float32


def dot_of(left, right, left_dim, right_dim):
    return lax.dot_general(
        left, right, (((left_dim,), (right_dim,)), ((), ())), preferred_element_type=F32
    )


def kernel_cost(microseconds):
    return pl.CostEstimate(
        flops=int(microseconds * 8e7), bytes_accessed=int(microseconds * 3e5), transcendentals=0
    )


def norm_scale(values):
    return lax.rsqrt(jnp.mean(values * values, axis=-1, keepdims=True) + EPSILON)


def bias_tiles_kernel(reversed_ref, tiles_ref):
    rows = tiles_ref.shape[1]
    width = reversed_ref.shape[2]
    for head in range(tiles_ref.shape[0]):
        line = jnp.broadcast_to(reversed_ref[head], (rows, width))
        skewed = pltpu.roll(line, width - (rows - 1), 1, stride=1, stride_axis=0)
        tiles_ref[head] = skewed[:, : tiles_ref.shape[2]]


def bias_tiles(reversed_bias, rows, columns):
    heads = reversed_bias.shape[0]
    return pl.pallas_call(
        bias_tiles_kernel,
        out_shape=jax.ShapeDtypeStruct((heads, rows, columns), F32),
        in_specs=[pl.BlockSpec(memory_space=pltpu.VMEM)],
        out_specs=pl.BlockSpec(memory_space=pltpu.VMEM),
        compiler_params=pltpu.CompilerParams(vmem_limit_bytes=VMEM_LIMIT),
        cost_estimate=kernel_cost(4),
        name="bias_tiles",
    )(reversed_bias)


def tile_start(me, key_block, query_block, ways, rows):
    key_place = lax.rem(me + key_block, ways)
    query_place = lax.rem(me + query_block, ways)
    return pl.multiple_of((query_place - key_place + ways - 1) * rows, rows)


def project_kernel(*refs):
    columns_ref, gain_ref, normed_ref, qkv_ref = refs[-4:]
    rows = refs[0].shape[1]
    columns = columns_ref[...].T
    for r, block_ref in enumerate(refs[:-4]):
        values = block_ref[0].astype(F32)
        normed = (values * norm_scale(values) * gain_ref[...]).astype(BF16)
        normed_ref[0, r * rows : (r + 1) * rows] = normed
        qkv_ref[0, :, r * rows : (r + 1) * rows] = dot_of(columns, normed, 1, 1).astype(BF16)


def project(blocks, columns, gain):
    seq_count, rows, model_width = blocks[0].shape
    length = rows * len(blocks)
    triple = columns.shape[1]
    return pl.pallas_call(
        project_kernel,
        grid=(seq_count,),
        out_shape=(
            jax.ShapeDtypeStruct((seq_count, length, model_width), BF16),
            jax.ShapeDtypeStruct((seq_count, triple, length), BF16),
        ),
        in_specs=[pl.BlockSpec((1, rows, model_width), lambda i: (i, 0, 0))] * len(blocks)
        + [
            pl.BlockSpec((model_width, triple), lambda i: (0, 0)),
            pl.BlockSpec((1, model_width), lambda i: (0, 0)),
        ],
        out_specs=(
            pl.BlockSpec((1, length, model_width), lambda i: (i, 0, 0)),
            pl.BlockSpec((1, triple, length), lambda i: (i, 0, 0)),
        ),
        compiler_params=pltpu.CompilerParams(vmem_limit_bytes=VMEM_LIMIT),
        cost_estimate=kernel_cost(5),
        name="project",
    )(*blocks, columns, gain)


def attend_kernel(me_ref, qkv_ref, tiles_ref, *refs):
    context_refs, total_ref, keys = refs[:-2], refs[-2], refs[-1]
    heads, rows = tiles_ref.shape[0], tiles_ref.shape[1]
    ways = len(context_refs)
    me = me_ref[0]
    for head in range(heads):
        first = 3 * head * HEAD
        keys[head] = qkv_ref[0, first + HEAD : first + 2 * HEAD].T
    for query_block in range(ways):
        query_rows = slice(query_block * rows, (query_block + 1) * rows)
        starts = [tile_start(me, place, query_block, ways, rows) for place in range(ways)]
        for head in range(heads):
            first = 3 * head * HEAD
            query = qkv_ref[0, first : first + HEAD, query_rows]
            scores = [
                dot_of(keys[head, place * rows : (place + 1) * rows], query, 1, 0)
                * (SCORE_SCALE * LOG2E)
                + tiles_ref[head, :, pl.ds(starts[place], rows)]
                for place in range(ways)
            ]
            top = scores[0]
            for tile in scores[1:]:
                top = jnp.maximum(top, tile)
            top = jnp.max(top, axis=0, keepdims=True)
            total = jnp.zeros((1, rows), F32)
            context = jnp.zeros((HEAD, rows), F32)
            for place in range(ways):
                value = qkv_ref[
                    0, first + 2 * HEAD : first + 3 * HEAD, place * rows : (place + 1) * rows
                ]
                shifted = jnp.exp2(scores[place] - top)
                total = total + jnp.sum(shifted, axis=0, keepdims=True)
                context = context + dot_of(value, shifted.astype(BF16), 1, 0)
            context_refs[query_block][0, head * HEAD : (head + 1) * HEAD] = (
                context / total
            ).astype(BF16)
            total_ref[0, head, :, query_rows] = top + jnp.log2(total)


def attend(me, qkv, tiles):
    seq_count, triple, length = qkv.shape
    heads, rows, columns = tiles.shape
    width, ways = triple // 3, length // rows
    results = pl.pallas_call(
        attend_kernel,
        grid=(seq_count,),
        out_shape=[jax.ShapeDtypeStruct((seq_count, width, rows), BF16)] * ways
        + [jax.ShapeDtypeStruct((seq_count, heads, 1, length), F32)],
        in_specs=[
            pl.BlockSpec(memory_space=pltpu.SMEM),
            pl.BlockSpec((1, triple, length), lambda i: (i, 0, 0)),
            pl.BlockSpec((heads, rows, columns), lambda i: (0, 0, 0)),
        ],
        out_specs=[pl.BlockSpec((1, width, rows), lambda i: (i, 0, 0))] * ways
        + [pl.BlockSpec((1, heads, 1, length), lambda i: (i, 0, 0, 0))],
        scratch_shapes=[pltpu.VMEM((heads, length, HEAD), BF16)],
        compiler_params=pltpu.CompilerParams(vmem_limit_bytes=32 * 1024 * 1024),
        cost_estimate=kernel_cost(11),
        name="attend",
    )(me, qkv, tiles)
    return results[:ways], results[ways]


def attend_back_kernel(me_ref, qkv_ref, *refs):
    ways = qkv_ref.shape[2] // refs[0].shape[2]
    grad_refs = refs[:ways]
    total_ref, tiles_ref = refs[ways : ways + 2]
    offset_ref, keys, values, key_sum, value_sum, tile_sum = refs[-6:]
    out_refs = refs[-6 - ways : -6]
    rows = tiles_ref.shape[1]
    me = me_ref[0]
    keys[...] = qkv_ref[0, HEAD : 2 * HEAD].T
    values[...] = qkv_ref[0, 2 * HEAD :].T
    key_sum[...] = jnp.zeros(key_sum.shape, F32)
    value_sum[...] = jnp.zeros(value_sum.shape, F32)
    tile_sum[...] = jnp.zeros(tile_sum.shape, F32)
    for query_block in range(ways):
        query_rows = slice(query_block * rows, (query_block + 1) * rows)
        starts = [tile_start(me, place, query_block, ways, rows) for place in range(ways)]
        query = qkv_ref[0, :HEAD, query_rows]
        grad = grad_refs[query_block][0]
        total = total_ref[0, 0, :, query_rows]
        probs, weight_grads = [], []
        inner = jnp.zeros((1, rows), F32)
        for place in range(ways):
            key_rows = slice(place * rows, (place + 1) * rows)
            scores = dot_of(keys[key_rows], query, 1, 0) * (SCORE_SCALE * LOG2E)
            prob = jnp.exp2(scores + (tiles_ref[0, :, pl.ds(starts[place], rows)] - total))
            weight_grad = dot_of(values[key_rows], grad, 1, 0)
            inner = inner + jnp.sum(prob * weight_grad, axis=0, keepdims=True)
            value_sum[:, key_rows] += dot_of(grad, prob.astype(BF16), 1, 1)
            probs.append(prob)
            weight_grads.append(weight_grad)
        query_grad = jnp.zeros((HEAD, rows), F32)
        for place in range(ways):
            key_rows = slice(place * rows, (place + 1) * rows)
            score_grad = probs[place] * (weight_grads[place] - inner)
            tile_sum[:, pl.ds(starts[place], rows)] += score_grad
            score_low = score_grad.astype(BF16)
            key_sum[:, key_rows] += dot_of(query, score_low, 1, 1)
            query_grad = query_grad + dot_of(
                qkv_ref[0, HEAD : 2 * HEAD, key_rows], score_low, 1, 0
            )
        out_refs[query_block][0, :HEAD] = (query_grad * SCORE_SCALE).astype(BF16)
    for place in range(ways):
        key_rows = slice(place * rows, (place + 1) * rows)
        out_refs[place][0, HEAD : 2 * HEAD] = (key_sum[:, key_rows] * SCORE_SCALE).astype(BF16)
        out_refs[place][0, 2 * HEAD :] = value_sum[:, key_rows].astype(BF16)
    folded, half = tile_sum[...], rows // 2
    while half:
        folded = pltpu.roll(folded[:half], half, 1) + folded[half:]
        half //= 2
    offset_ref[0] = folded


def attend_back(me, qkv, grads, totals, tiles, span, head, earlier):
    seq_count, _, length = qkv.shape
    _, rows, columns = tiles.shape
    ways = length // rows
    results = pl.pallas_call(
        attend_back_kernel,
        grid=(seq_count,),
        out_shape=[jax.ShapeDtypeStruct((seq_count, 3 * HEAD, rows), BF16)] * ways
        + [jax.ShapeDtypeStruct((seq_count, 1, span), F32)],
        in_specs=[
            pl.BlockSpec(memory_space=pltpu.SMEM),
            pl.BlockSpec((1, 3 * HEAD, length), lambda i: (i, head, 0)),
        ]
        + [pl.BlockSpec((1, HEAD, rows), lambda i: (i, head, 0))] * ways
        + [
            pl.BlockSpec((1, 1, 1, length), lambda i: (i, head, 0, 0)),
            pl.BlockSpec((1, rows, columns), lambda i: (head, 0, 0)),
        ]
        + [pl.BlockSpec(memory_space=pl.ANY)] * len(earlier),
        out_specs=[pl.BlockSpec((1, 3 * HEAD, rows), lambda i: (i, 0, 0))] * ways
        + [pl.BlockSpec((1, 1, span), lambda i: (i, 0, 0))],
        scratch_shapes=[
            pltpu.VMEM((length, HEAD), BF16),
            pltpu.VMEM((length, HEAD), BF16),
            pltpu.VMEM((HEAD, length), F32),
            pltpu.VMEM((HEAD, length), F32),
            pltpu.VMEM((rows, span), F32),
        ],
        compiler_params=pltpu.CompilerParams(vmem_limit_bytes=24 * 1024 * 1024),
        cost_estimate=kernel_cost(80),
        name="attend_back",
    )(me, qkv, *grads, totals, tiles, *earlier)
    return results[:ways], results[ways]


def column_kernel(normed_ref, columns_ref, *refs):
    ways = normed_ref.shape[1] // refs[0].shape[2]
    heads = columns_ref.shape[1] // refs[0].shape[1]
    grad_refs = refs[: heads * ways]
    out_ref, gain_ref = refs[-2:]
    rows = refs[0].shape[2]
    parts = []
    for head in range(heads):
        part = 0.0
        for seq in range(normed_ref.shape[0]):
            for r in range(ways):
                part += dot_of(
                    grad_refs[head * ways + r][seq],
                    normed_ref[seq, r * rows : (r + 1) * rows],
                    1,
                    0,
                )
        parts.append(part)
    total = jnp.concatenate(parts, axis=0).T
    out_ref[...] = total.astype(BF16)
    gain_ref[...] = jnp.sum(total * columns_ref[...].astype(F32), axis=1, keepdims=True)


def column_grads(normed, columns, grads, earlier):
    count = 2 + len(grads)
    return pl.pallas_call(
        column_kernel,
        out_shape=(
            jax.ShapeDtypeStruct(columns.shape, BF16),
            jax.ShapeDtypeStruct((columns.shape[0], 1), F32),
        ),
        in_specs=[pl.BlockSpec(memory_space=pltpu.VMEM)] * count
        + [pl.BlockSpec(memory_space=pl.ANY)] * len(earlier),
        out_specs=[pl.BlockSpec(memory_space=pltpu.VMEM)] * 2,
        compiler_params=pltpu.CompilerParams(vmem_limit_bytes=VMEM_LIMIT),
        cost_estimate=kernel_cost(5),
        name="column_grads",
    )(normed, columns, *grads, *earlier)


def token_grads(me, tokens, hidden_grad, gain, weights, first_block, moved, earlier):
    seq_count, rows, model_width = tokens.shape
    shards = weights.shape[0]
    own_rows = model_width // shards
    local_heads, ways = len(moved), len(moved[0])
    grads = [grad for blocks in moved for grad in blocks]
    block = pl.BlockSpec((1, rows, model_width), lambda i: (i, 0, 0))

    def kernel(me_ref, tokens_ref, hidden_grad_ref, gain_ref, *refs):
        weight_refs, grad_refs = refs[:3], refs[3 : 3 + len(grads)]
        out_ref, gathered = refs[-2:]
        for head in range(local_heads):
            for r in range(ways):
                place = lax.rem(me_ref[0] - r + ways, ways) * local_heads + head
                place = pl.multiple_of(place * HEAD, HEAD)
                for kind in range(3):
                    gathered[kind, pl.ds(place, HEAD)] = grad_refs[head * ways + r][
                        0, kind * HEAD : (kind + 1) * HEAD
                    ]
        normed_grad = 0.0
        for kind in range(3):
            weight = weight_refs[kind][...].reshape(model_width, model_width)
            normed_grad += dot_of(gathered[kind], weight, 0, 1)
        inputs = tokens_ref[0].astype(F32)
        scale = norm_scale(inputs)
        weighted = normed_grad * gain_ref[...]
        inner_sum = jnp.mean(weighted * inputs, axis=-1, keepdims=True)
        out_ref[0] = (
            hidden_grad_ref[0] + scale * weighted - inputs * (scale * scale * scale) * inner_sum
        )

    def weight_spec(place):
        return pl.BlockSpec((shards, own_rows, model_width), lambda i: (0, place, 0))

    weights, weight_specs = [weights] * 3, [weight_spec(first_block + kind) for kind in range(3)]
    if own_rows % 16:
        weights = [
            weights[0][:, (first_block + kind) * own_rows : (first_block + kind + 1) * own_rows]
            for kind in range(3)
        ]
        weight_specs = [weight_spec(0)] * 3
    return pl.pallas_call(
        kernel,
        grid=(seq_count,),
        out_shape=jax.ShapeDtypeStruct(tokens.shape, F32),
        in_specs=[
            pl.BlockSpec(memory_space=pltpu.SMEM),
            block,
            block,
            pl.BlockSpec((1, model_width), lambda i: (0, 0)),
        ]
        + weight_specs
        + [pl.BlockSpec((1,) + grads[0].shape[1:], lambda i: (i, 0, 0))] * len(grads)
        + [pl.BlockSpec(memory_space=pl.ANY)] * len(earlier),
        out_specs=block,
        scratch_shapes=[pltpu.VMEM((3, model_width, rows), BF16)],
        compiler_params=pltpu.CompilerParams(vmem_limit_bytes=24 * 1024 * 1024),
        cost_estimate=kernel_cost(6),
        name="token_grads",
    )(me, tokens, hidden_grad, gain, *weights, *grads, *earlier)


def out_grads(places, contexts, grads, ways, shards, earlier):
    seq_count, model_width, rows = contexts.shape
    width, per_group = model_width // ways, shards // ways
    own_rows = model_width // shards

    def kernel(places_ref, contexts_ref, grads_ref, *refs):
        kept_ref, sent_ref = refs[-2:]
        even = places_ref[1] % 2 == 0
        for r in range(ways):
            part = 0.0
            for seq in range(seq_count):
                part += dot_of(
                    contexts_ref[seq, r * width : (r + 1) * width], grads_ref[seq], 1, 0
                )
            pairs = part.reshape(per_group // 2, 2, own_rows, model_width)
            group = lax.rem(places_ref[0] - r + ways, ways)
            place = pl.ds(group * (per_group // 2), per_group // 2)
            kept_ref[place] = jnp.where(even, pairs[:, 0], pairs[:, 1]).astype(BF16)
            sent_ref[place] = jnp.where(even, pairs[:, 1], pairs[:, 0]).astype(BF16)

    return pl.pallas_call(
        kernel,
        out_shape=[jax.ShapeDtypeStruct((shards // 2, own_rows, model_width), BF16)] * 2,
        in_specs=[pl.BlockSpec(memory_space=pltpu.SMEM)]
        + [pl.BlockSpec(memory_space=pltpu.VMEM)] * 2
        + [pl.BlockSpec(memory_space=pl.ANY)] * len(earlier),
        out_specs=[pl.BlockSpec(memory_space=pltpu.VMEM)] * 2,
        compiler_params=pltpu.CompilerParams(vmem_limit_bytes=VMEM_LIMIT),
        cost_estimate=kernel_cost(3),
        name="out_grads",
    )(places, contexts, grads, *earlier)


def experts_kernel(*refs):
    weights_ref = refs[6]
    slots, plain, gates = [
        jnp.concatenate([refs[k][0], refs[k + 1][0]], axis=0) for k in (0, 2, 4)
    ]
    plain = plain.astype(F32)
    grads = (plain * gates).astype(BF16)
    shards, rows, model_width = weights_ref.shape
    units = rows // 2
    up = weights_ref[:, :units].reshape(shards * units, model_width)
    down = weights_ref[:, units:].reshape(shards * units, model_width)
    pre = dot_of(slots, up, 1, 1)
    normal_cdf = 0.5 * (1.0 + lax.erf(pre * ROOT_HALF))
    act = (pre * normal_cdf).astype(BF16)
    slope = normal_cdf + pre * jnp.exp(-0.5 * pre * pre) * DENSITY
    act_grad = dot_of(grads, down, 1, 1)
    pre_grad = (act_grad * slope).astype(BF16)
    returned = dot_of(act, down, 1, 0)
    back = dot_of(pre_grad, up, 1, 0)
    if len(refs) == 10:
        out_ref, back_ref, parts_ref = refs[7:]
        out_ref[0] = returned
        back_ref[0] = back
    else:
        out_ref, far_out_ref, back_ref, far_back_ref, gate_ref, far_gate_ref, parts_ref = refs[10:]
        half = slots.shape[0] // 2
        returned += refs[7][0]
        back += refs[8][0]
        gate_parts = jnp.sum(returned * plain, axis=1, keepdims=True)
        out_ref[0] = returned[:half].astype(BF16)
        far_out_ref[0] = returned[half:].astype(BF16)
        back_ref[0] = back[:half].astype(BF16)
        far_back_ref[0] = back[half:].astype(BF16)
        gate_ref[0] = gate_parts[:half]
        far_gate_ref[0] = gate_parts[half:]
    part_shape = (shards, units, model_width)
    parts_ref[:, :units] = dot_of(pre_grad, slots, 0, 0).astype(BF16).reshape(part_shape)
    parts_ref[:, units:] = dot_of(act, grads, 0, 0).astype(BF16).reshape(part_shape)


def experts(slots, grads, gates, weights, units, before):
    expert_count, rows, model_width = slots[0].shape
    shards = weights.shape[0]
    row_spec = pl.BlockSpec((1, rows, model_width), lambda e: (e, 0, 0))
    gate_spec = pl.BlockSpec((1, rows, 1), lambda e: (e, 0, 0))
    both_spec = pl.BlockSpec((1, 2 * rows, model_width), lambda e: (e, 0, 0))
    weight_block = (shards, 2 * units, model_width)
    place = expert_count if before else 0
    both = jax.ShapeDtypeStruct((expert_count, 2 * rows, model_width), F32)
    half = jax.ShapeDtypeStruct((expert_count, rows, model_width), BF16)
    gate = jax.ShapeDtypeStruct((expert_count, rows, 1), F32)
    parts = jax.ShapeDtypeStruct((shards, 4 * expert_count * units, model_width), BF16)
    parts_spec = pl.BlockSpec(weight_block, lambda e: (0, place + e, 0))
    return pl.pallas_call(
        experts_kernel,
        grid=(expert_count,),
        out_shape=[half] * 4 + [gate] * 2 + [parts] if before else [both] * 2 + [parts],
        in_specs=[row_spec] * 4
        + [gate_spec] * 2
        + [pl.BlockSpec(weight_block, lambda e: (0, e, 0))]
        + ([both_spec, both_spec, pl.BlockSpec(memory_space=pl.ANY)] if before else []),
        out_specs=(
            [row_spec] * 4 + [gate_spec] * 2 + [parts_spec]
            if before
            else [both_spec] * 2 + [parts_spec]
        ),
        input_output_aliases={9: 6} if before else {},
        compiler_params=pltpu.CompilerParams(vmem_limit_bytes=VMEM_LIMIT),
        cost_estimate=kernel_cost(9),
        name="experts",
    )(*slots, *grads, *gates, weights, *before)


def turned(values, axis_name, step):
    ways = lax.axis_size(axis_name)
    return lax.ppermute(values, axis_name, [((i + step) % ways, i) for i in range(ways)])


def following_kernel(*refs):
    pass


def following(values, *earlier):
    anywhere = pl.BlockSpec(memory_space=pl.ANY)
    return pl.pallas_call(
        following_kernel,
        out_shape=jax.ShapeDtypeStruct(values.shape, values.dtype),
        in_specs=[anywhere] * (1 + len(earlier)),
        out_specs=anywhere,
        input_output_aliases={0: 0},
        cost_estimate=kernel_cost(1),
        name="following",
    )(values, *earlier)


def flipped(values, axis_name, bit):
    ways = lax.axis_size(axis_name)
    return lax.ppermute(values, axis_name, [(i, i ^ (1 << bit)) for i in range(ways)])


def sum_everywhere(values, axis_names):
    for axis_name in axis_names:
        for bit in range(lax.axis_size(axis_name).bit_length() - 1):
            values = values + flipped(values, axis_name, bit)
    return values


def scattered_steps(values, axis_name, order, waits):
    steps, left = [], sorted(order, reverse=True)
    place = jnp.full((1,), lax.axis_index(axis_name), jnp.int32)
    parts = values.reshape((2,) * len(order) + (-1,) + values.shape[1:])
    for bit in order:
        if bit in waits:
            place = following(place, *waits[bit])
        mine = (place[0] >> bit) & 1
        axis = left.index(bit)
        left.remove(bit)
        kept = lax.dynamic_index_in_dim(parts, mine, axis, keepdims=False)
        sent = lax.dynamic_index_in_dim(parts, 1 - mine, axis, keepdims=False)
        received = flipped(sent, axis_name, bit)
        parts = (kept.astype(F32) + received.astype(F32)).astype(values.dtype)
        steps.append(parts)
    return steps


def cyclic(values, me, ways, axis, direction):
    size = values.shape[axis] // ways
    return jnp.concatenate(
        [
            lax.dynamic_slice_in_dim(
                values, lax.rem(me + direction * r + ways, ways) * size, size, axis
            )
            for r in range(ways)
        ],
        axis=axis,
    )


def shards(
    tokens,
    routes,
    buckets,
    gain_attn,
    w_query,
    w_key,
    w_value,
    w_out,
    bias_table,
    gain_ff,
    router,
    expert_up,
    expert_down,
    out_grad,
):
    seq_count, block_rows, model_width = tokens.shape
    ways = lax.axis_size("seq")
    group = lax.axis_size("fsdp")
    me = lax.axis_index("seq")
    length = block_rows * ways
    capacity = block_rows * 9 // 16
    expert_count = router.shape[1]
    token_rows = seq_count * block_rows
    slot_rows = seq_count * capacity
    width = model_width // ways
    local_heads = width // HEAD
    places = jnp.full((1,), me, jnp.int32)

    others = [turned(tokens, "seq", r) for r in range(1, ways)]

    def columns_of(place):
        parts = [
            lax.dynamic_slice_in_dim(weight, place * width, width, 1).reshape(-1, local_heads, HEAD)
            for weight in (w_query, w_key, w_value)
        ]
        return jnp.stack(parts, axis=2).reshape(-1, 3 * width)

    own_columns = lax.all_gather(columns_of(me), "fsdp", axis=0, tiled=True)

    units = expert_up.shape[1]
    expert_rows = 2 * expert_count * units
    own_rows = w_out.shape[0]
    own_experts = jnp.stack([expert_up, expert_down], axis=1).reshape(expert_rows, model_width)
    own_weights = lax.all_gather(
        jnp.concatenate([own_experts, w_out, w_query, w_key, w_value]), "fsdp", axis=0
    )
    out_cyclic = cyclic(
        own_weights[:, expert_rows : expert_rows + own_rows].reshape(model_width, model_width),
        me, ways, 0, -1,
    )

    chosen = routes[:, :, 0]
    picked = (chosen[:, :, None] == jnp.arange(expert_count)[None, None, :]).astype(F32)
    earlier = jnp.cumsum(picked, axis=1) - picked
    slot_number = jnp.sum(earlier * picked, axis=-1).astype(jnp.int32)
    slot_index = chosen * capacity + slot_number
    dispatch = (
        slot_index[:, None, :] == jnp.arange(expert_count * capacity)[None, :, None]
    ).reshape(seq_count, expert_count, capacity, block_rows)
    dispatch_low = dispatch.astype(BF16)

    def to_slots(values):
        placed = jnp.einsum("nect,ntd->encd", dispatch_low, values, preferred_element_type=F32)
        return placed.astype(BF16).reshape(expert_count, slot_rows, model_width)

    def from_slots(values):
        return jnp.einsum(
            "nect,encd->ntd",
            dispatch_low,
            values.astype(BF16).reshape(expert_count, seq_count, capacity, model_width),
            preferred_element_type=F32,
        )

    grad_slots = to_slots(out_grad)
    far_grad_slots = flipped(grad_slots, "seq", 0)

    table_here = lax.dynamic_slice_in_dim(bias_table, me * local_heads, local_heads, 1)
    bucket_table = (buckets[:, None] == jnp.arange(bias_table.shape[0])[None, :]).astype(F32)
    reversed_buckets = jnp.pad(bucket_table[::-1], ((0, 1), (0, 0)))
    reversed_bias = jnp.einsum(
        "uk,kh->hu", reversed_buckets, table_here * LOG2E, precision=PRECISE
    )
    tiles = bias_tiles(reversed_bias[:, None, :], block_rows, length * 2 - block_rows)

    far_experts = flipped(
        following(
            own_experts, *others, own_columns, tiles
        ),
        "seq",
        1,
    )
    normed_all, qkv = project(
        [tokens] + others, own_columns, gain_attn[None]
    )
    contexts, totals = attend(places, qkv, tiles)
    far_weights = lax.all_gather(following(far_experts, contexts[0]), "fsdp", axis=0)
    context_t = jnp.concatenate(
        [contexts[0]] + [turned(contexts[r], "seq", -r) for r in range(1, ways)], axis=1
    )
    attn_branch = jnp.einsum("nct,cd->ntd", context_t, out_cyclic, preferred_element_type=F32)
    inputs = tokens.astype(F32)
    hidden = inputs + attn_branch
    second_scale = norm_scale(hidden)
    ffnorm = hidden * second_scale * gain_ff
    logits = jnp.einsum("std,de->ste", ffnorm, router, precision=PRECISE)
    route_probs = jax.nn.softmax(logits, axis=-1)
    gate_value = jnp.sum(route_probs * picked, axis=-1)

    slots = to_slots(ffnorm.astype(BF16))
    gate_slots = jnp.einsum(
        "nect->enc", jnp.where(dispatch, gate_value[:, None, None, :], 0.0)
    ).reshape(expert_count, slot_rows)
    far_slots = flipped(slots, "seq", 0)
    far_gate_slots = flipped(gate_slots, "seq", 0)
    given = (
        (slots, far_slots),
        (grad_slots, far_grad_slots),
        (gate_slots[..., None], far_gate_slots[..., None]),
    )
    before = experts(*given, own_weights, units, ())
    returned, far_returned, slot_back, far_back, gate_parts, far_gate_parts, parts = experts(
        *given, far_weights, units, before
    )
    expert_share = lax.psum_scatter(parts, "fsdp", scatter_dimension=0, tiled=True)[0]
    moved_share = flipped(expert_share[expert_rows:], "seq", 1)
    gate_grad_slots = gate_parts[..., 0] + flipped(far_gate_parts[..., 0], "seq", 0)
    slot_sum = slot_back.astype(F32) + flipped(far_back, "seq", 0).astype(F32)
    upstream = out_grad.astype(F32)
    gate_grad = jnp.sum(
        jnp.where(
            dispatch,
            gate_grad_slots.reshape(expert_count, seq_count, capacity).transpose(1, 0, 2)[..., None],
            0.0,
        ),
        axis=(1, 2),
    )
    logit_grad = gate_value[:, :, None] * (picked - route_probs) * gate_grad[:, :, None]
    ffnorm_grad = from_slots(slot_sum) + jnp.einsum(
        "ste,de->std", logit_grad, router, precision=PRECISE
    )
    router_grad = jnp.einsum("std,ste->de", ffnorm, logit_grad, precision=PRECISE)
    weighted = ffnorm_grad * gain_ff
    inner_sum = jnp.mean(weighted * hidden, axis=-1, keepdims=True)
    hidden_grad = (
        upstream + second_scale * weighted - hidden * (second_scale**3) * inner_sum
    )
    gain_ff_grad = jnp.sum(ffnorm_grad * hidden * second_scale, axis=(0, 1))
    branch_grad = hidden_grad.astype(BF16)
    context_grad = jnp.einsum(
        "cd,ntd->nct", out_cyclic, branch_grad, preferred_element_type=F32
    ).astype(BF16)
    context_grads = [context_grad[:, :width]] + [
        turned(context_grad[:, r * width : (r + 1) * width], "seq", r) for r in range(1, ways)
    ]
    group = lax.axis_size("fsdp")
    out_kept, out_sent = out_grads(
        jnp.stack([me, lax.axis_index("fsdp")]).astype(jnp.int32), context_t, branch_grad, ways, group,
        [],
    )
    out_half = (out_kept.astype(F32) + flipped(out_sent, "fsdp", 0).astype(F32)).astype(BF16)
    bits = list(range(1, group.bit_length() - 1))
    out_steps = [out_half] + scattered_steps(out_half, "fsdp", bits, {})
    out_steps[-1] = out_steps[-1].reshape(-1, model_width)
    far_returned = flipped(following(far_returned, *context_grads[1:]), "seq", 0)
    returned_sum = returned.astype(F32) + far_returned.astype(F32)
    output = (hidden + gate_value[:, :, None] * from_slots(returned_sum)).astype(BF16)
    out_share = out_steps[-1]
    out_pair = out_share.astype(F32) + flipped(out_share, "seq", 0).astype(F32)
    out_pair = out_pair.astype(BF16)
    far_pair = flipped(out_pair, "seq", 1)
    out_sum = out_pair.astype(F32) + far_pair.astype(F32)

    head_grads, moved_grads, offset_grads = [], [], []
    for head in range(local_heads):
        earlier = out_steps[head : head + 1] if head else []
        if head > 1:
            earlier = earlier + moved_grads[head - 2][1:] + [far_returned]
        head_grad, offset_grad = attend_back(
            places, qkv, context_grads, totals, tiles, 2 * length, head, earlier
        )
        head_grads += head_grad
        moved_grads.append(
            [head_grad[0]] + [turned(head_grad[r], "seq", -r) for r in range(1, ways)]
        )
        offset_grads.append(jnp.sum(offset_grad, axis=0))
    column_grad, gain_attn_part = column_grads(
        normed_all, own_columns, head_grads, moved_grads[-2][1:] + [out_pair]
    )
    gain_attn_part = gain_attn_part[:, 0] / gain_attn
    column_steps = scattered_steps(
        column_grad, "fsdp", [0] + bits, {}
    )
    column_share = column_steps[-1].reshape(-1, 3 * width)
    tokens_grad = token_grads(
        places, tokens, hidden_grad, gain_attn[None], own_weights, expert_rows // own_rows + 1,
        moved_grads, [column_grad],
    )

    table_part = jnp.einsum(
        "uk,hu->kh", reversed_buckets, jnp.concatenate(offset_grads, axis=0), precision=PRECISE
    )
    table_full = lax.dynamic_update_slice_in_dim(
        jnp.zeros(bias_table.shape, F32), table_part, me * local_heads, 1
    )
    small = jnp.concatenate(
        [gain_attn_part, gain_ff_grad, router_grad.reshape(-1), table_full.reshape(-1)]
    )
    small = sum_everywhere(small, ("fsdp",))
    small = sum_everywhere(following(small, moved_share), ("seq",))
    column_share = following(column_share, moved_share, tokens_grad)
    gain_attn_sum = small[:model_width]
    gain_ff_sum = small[model_width : 2 * model_width]
    router_sum = small[2 * model_width : 2 * model_width + router.size].reshape(router.shape)
    table_sum = small[2 * model_width + router.size :].reshape(bias_table.shape)

    expert_sum = expert_share[:expert_rows].astype(F32) + moved_share.astype(F32)
    expert_sum = expert_sum.reshape(expert_count, 2, units, model_width)
    column_shares = jnp.concatenate(
        [column_share] + [turned(column_share, "seq", r) for r in range(1, ways)], axis=1
    )
    column_shares = cyclic(column_shares, ways - me, ways, 1, 1).astype(F32)
    column_shares = column_shares.reshape(-1, ways * local_heads, 3, HEAD)
    attn_sums = [column_shares[:, :, kind].reshape(-1, model_width) for kind in range(3)]
    return (
        output,
        tokens_grad,
        gain_attn_sum,
        attn_sums[0],
        attn_sums[1],
        attn_sums[2],
        out_sum,
        table_sum,
        gain_ff_sum,
        router_sum,
        expert_sum[:, 0],
        expert_sum[:, 1],
    )


def solution(mesh):
    in_specs = (
        P("fsdp", "seq", None),
        P("fsdp", "seq", None),
        P(),
        P(),
        P("fsdp", None),
        P("fsdp", None),
        P("fsdp", None),
        P("fsdp", None),
        P(),
        P(),
        P(),
        P(None, ("seq", "fsdp"), None),
        P(None, ("seq", "fsdp"), None),
        P("fsdp", "seq", None),
    )
    out_specs = (
        P("fsdp", "seq", None),
        P("fsdp", "seq", None),
        P(),
        P("fsdp", None),
        P("fsdp", None),
        P("fsdp", None),
        P("fsdp", None),
        P(),
        P(),
        P(),
        P(None, ("seq", "fsdp"), None),
        P(None, ("seq", "fsdp"), None),
    )
    return jax.shard_map(shards, mesh=mesh, in_specs=in_specs, out_specs=out_specs, check_vma=False)
```
